32 devices in a mesh: grp: 2 (over x), blk: 16 (over z, y, core).
Axes of the slice: x: 2, y: 2, z: 4, core: 2. Of those that a mesh axis runs over, the one named last changes fastest.
Arguments:
- zonal_velocity_field: bfloat16 [512, 64, 128], P('blk'), may hold values from -6 to 6
- meridional_velocity_field: bfloat16 [512, 64, 128], P('blk'), may hold values from -6 to 6
- barometric_disturbance: bfloat16 [512, 64, 128], P('blk'), may hold values from -6 to 6
- delayed_thermal_deviation: bfloat16 [512, 64, 128], P('blk'), may hold values from -6 to 6
- delayed_moisture_deviation: bfloat16 [512, 64, 128], P('blk'), may hold values from -6 to 6
- flow_category_label: int32 [512, 64], P('blk'), may hold values from 0 to 15, as said below
- advective_stability_number: float32 [128], replicated, may hold values from 0.25 to 1.3
- initial_dense_matrix: bfloat16 [16, 256, 1024], P('blk'), may hold values from -0.5 to 0.5
- middle_dense_matrix: bfloat16 [16, 1024, 1024], P('blk'), may hold values from -0.25 to 0.25
- closing_dense_matrix: bfloat16 [16, 1024, 1024], P('blk'), may hold values from -0.25 to 0.25
- final_readout_matrix: bfloat16 [16, 1024, 256], P('blk'), may hold values from -0.25 to 0.25
Outputs:
- new_east: bfloat16 [512, 64, 128], P('blk', 'grp')
- new_north: bfloat16 [512, 64, 128], P('blk', 'grp')
- new_pressure: bfloat16 [512, 64, 128], P('blk', 'grp')
- heating: bfloat16 [512, 64, 128], P('blk', 'grp')
- moistening: bfloat16 [512, 64, 128], P('blk', 'grp')
The draws below stay inside these ranges and needn't reach their ends.
Inputs may be any that keep to these rules, and one draw needn't show every extreme that they name: Each tile block, rows 32 * b to 32 * b + 31 of flow_category_label, holds exactly 128 columns of every regime.
All inputs are finite; a program needn't handle non-finite values.
Results may differ from the reference program's by a relative error of at most 0.012.
Values may be sent and summed in bfloat16 or wider, within the bound.
No kernel may reach another device: no remote copies, remote signals or barrier semaphores. Data moves between devices by JAX's collectives and lax.ppermute only.
A program may use at most 64 MiB of HBM per device.

```python
import math
import jax
import jax.numpy as jnp
from jax import lax

CX = 32
MERIDIAN_COUNT = 64
HEIGHT_COUNT = 128
HID = 1024
SUB = 4
ZONAL_COUNT = 512
REGIMES = 16


def draw_flow_category_label(key, part):
    blocks = ZONAL_COUNT // CX
    per_block = CX * MERIDIAN_COUNT
    share = per_block // blocks
    block_keys = jax.random.split(jax.random.fold_in(key, 17), blocks)
    shuffled = jax.vmap(lambda block_key: jax.random.permutation(block_key, per_block))(block_keys)
    return (shuffled // share).astype(jnp.int32).reshape(blocks * CX, MERIDIAN_COUNT)


def level_of(rng, extent, cuts, least, high):
    level, own = 1.0, jax.random.fold_in(rng, 6)
    for axis_at, shards_of in cuts:
        steps = jnp.exp(jax.random.uniform(jax.random.fold_in(own, axis_at), (shards_of,), jnp.float32, least / len(cuts), high / len(cuts)))
        level = level * jnp.repeat(steps, extent[axis_at] // shards_of).reshape([-1 if axis == axis_at else 1 for axis in range(len(extent))])
    return level


def gaussian(key, shape, spread, bound, pieces=(), kind=jnp.bfloat16):
    array = jax.random.normal(key, shape, jnp.float32) * spread
    if len(pieces) > 0:
        array = level_of(key, shape, pieces, -0.22, 0.18) * array
    return jnp.clip(array, min=-bound, max=bound).astype(kind)


def setup_inputs(seed: int = 0) -> dict:
    keys = jax.random.split(jax.random.key(seed), 12)
    return {
        "zonal_velocity_field": gaussian(keys[0], (ZONAL_COUNT, MERIDIAN_COUNT, HEIGHT_COUNT), 1.0, 6.0, ((0, 16),)),
        "meridional_velocity_field": gaussian(keys[1], (ZONAL_COUNT, MERIDIAN_COUNT, HEIGHT_COUNT), 1.0, 6.0, ((0, 16),)),
        "barometric_disturbance": gaussian(keys[2], (ZONAL_COUNT, MERIDIAN_COUNT, HEIGHT_COUNT), 1.0, 6.0, ((0, 16),)),
        "delayed_thermal_deviation": gaussian(keys[3], (ZONAL_COUNT, MERIDIAN_COUNT, HEIGHT_COUNT), 1.0, 6.0, ((0, 16),)),
        "delayed_moisture_deviation": gaussian(keys[4], (ZONAL_COUNT, MERIDIAN_COUNT, HEIGHT_COUNT), 1.0, 6.0, ((0, 16),)),
        "flow_category_label": draw_flow_category_label(jax.random.fold_in(keys[11], 71), 0),
        "advective_stability_number": jnp.clip(jnp.exp(jax.random.uniform(keys[6], (HEIGHT_COUNT,), jnp.float32, math.log(0.25), math.log(1.3))), 0.25, 1.3),
        "initial_dense_matrix": gaussian(keys[7], (REGIMES, 2 * HEIGHT_COUNT, HID), HEIGHT_COUNT ** -0.5, 0.5, ((0, 16),)),
        "middle_dense_matrix": gaussian(keys[8], (REGIMES, HID, HID), (HID // 2) ** -0.5, 0.25, ((0, 16),)),
        "closing_dense_matrix": gaussian(keys[9], (REGIMES, HID, HID), (HID // 2) ** -0.5, 0.25, ((0, 16),)),
        "final_readout_matrix": gaussian(keys[10], (REGIMES, HID, 2 * HEIGHT_COUNT), (HID // 2) ** -0.5, 0.25, ((0, 16),)),
    }


def along_cycle(field):
    return (jnp.roll(field, -1, 0) - jnp.roll(field, 1, 0)) * 0.5


def across_belt(field):
    padded = jnp.pad(field, ((0, 0), (1, 1), (0, 0)))
    return (padded[:, 2:] - padded[:, :-2]) * 0.5


def network(inputs):
    columns, first, second, third, last = inputs
    hidden = jax.nn.silu(jnp.dot(columns, first, preferred_element_type=jnp.float32)).astype(jnp.bfloat16)
    hidden = jax.nn.silu(jnp.dot(hidden, second, preferred_element_type=jnp.float32)).astype(jnp.bfloat16)
    hidden = jax.nn.silu(jnp.dot(hidden, third, preferred_element_type=jnp.float32)).astype(jnp.bfloat16)
    return jnp.dot(hidden, last, preferred_element_type=jnp.float32).astype(jnp.bfloat16)


def reference(zonal_velocity_field, meridional_velocity_field, barometric_disturbance, delayed_thermal_deviation, delayed_moisture_deviation, flow_category_label, advective_stability_number, initial_dense_matrix, middle_dense_matrix, closing_dense_matrix, final_readout_matrix):
    courant_rate = advective_stability_number.astype(jnp.float32)
    eastward = zonal_velocity_field.astype(jnp.float32)
    northward = meridional_velocity_field.astype(jnp.float32)
    pressure_state = barometric_disturbance.astype(jnp.float32)
    for substep in range(SUB):
        eastward = eastward - courant_rate * along_cycle(pressure_state)
        northward = northward - courant_rate * across_belt(pressure_state)
        pressure_state = pressure_state - courant_rate * (along_cycle(eastward) + across_belt(northward))
    atmosphere_soundings = jnp.concatenate([delayed_thermal_deviation, delayed_moisture_deviation], axis=-1).reshape(ZONAL_COUNT * MERIDIAN_COUNT, 2 * HEIGHT_COUNT)
    sorting = jnp.argsort(flow_category_label.reshape(-1), stable=True)
    batches = jnp.take(atmosphere_soundings, sorting, axis=0).reshape(REGIMES, (ZONAL_COUNT * MERIDIAN_COUNT) // REGIMES, 2 * HEIGHT_COUNT)
    results = lax.map(network, (batches, initial_dense_matrix, middle_dense_matrix, closing_dense_matrix, final_readout_matrix))
    placed = jnp.zeros_like(atmosphere_soundings).at[sorting].set(results.reshape(ZONAL_COUNT * MERIDIAN_COUNT, 2 * HEIGHT_COUNT))
    tendency = placed.reshape(ZONAL_COUNT, MERIDIAN_COUNT, 2 * HEIGHT_COUNT)
    return (eastward.astype(jnp.bfloat16), northward.astype(jnp.bfloat16), pressure_state.astype(jnp.bfloat16), tendency[:, :, :HEIGHT_COUNT], tendency[:, :, HEIGHT_COUNT:])
```

```python
import functools
import jax
import jax.numpy as jnp
from jax import lax
from jax.experimental import pallas as pl
from jax.experimental.pallas import tpu as pltpu
from jax.sharding import PartitionSpec as P

SUB = 4
CHUNKS = 2
LANES = 128
MIB = 1 << 20
bf16, f32, i32 = jnp.bfloat16, jnp.float32, jnp.int32


def params(mib):
    return pltpu.CompilerParams(vmem_limit_bytes=mib * MIB)


def cost(flops, moved):
    return pl.CostEstimate(flops=flops, bytes_accessed=moved, transcendentals=0)


def folded(labels, start, half):
    rows = labels.shape[0] * half // LANES
    side = labels[:, start : start + half]
    return jnp.concatenate(
        [side[t * rows : (t + 1) * rows] for t in range(LANES // half)], axis=1
    )


def ranked(labels, regimes):
    rows = labels.shape[0]
    shape = (regimes, rows, LANES)
    member = jnp.where(
        lax.broadcasted_iota(i32, shape, 0) == jnp.broadcast_to(labels[None], shape), 1.0, 0.0
    )
    flat = member.reshape(regimes * rows, LANES).astype(bf16)
    first = lax.broadcasted_iota(i32, (LANES, LANES), 0)
    second = lax.broadcasted_iota(i32, (LANES, LANES), 1)
    earlier = jnp.where(first < second, 1.0, 0.0).astype(bf16)
    within = jnp.dot(flat, earlier, preferred_element_type=f32).reshape(shape)
    totals = jnp.dot(
        flat, jnp.ones((LANES, LANES), bf16), preferred_element_type=f32
    ).reshape(shape)
    before = jnp.zeros((regimes, 1, LANES), f32)
    rank = jnp.zeros((rows, LANES), f32)
    row_ranks = []
    for m in range(rows):
        row_ranks.append(
            jnp.sum(member[:, m : m + 1] * (within[:, m : m + 1] + before), axis=0)
        )
        before = before + totals[:, m : m + 1]
    rank = jnp.concatenate(row_ranks, axis=0)
    return rank, member, before


def route_kernel(regimes, part, group_ref, label_ref, heat_ref, moist_ref, *out_refs):
    labels = label_ref[...]
    deep, wide = labels.shape
    half = wide // 2
    rows = deep * half // LANES
    mine = group_ref[0]
    width = part // len(out_refs)
    slots = []
    for side in range(2):
        index = folded(labels, side * half, half)
        rank, _, _ = ranked(index, regimes)
        place = jnp.where(mine == side, part - 1.0 - rank, rank - part)
        slots.append((place, index.astype(f32) * width))
    columns = []
    for side in range(2):
        for m in range(rows):
            for t in range(LANES // half):
                at = (m + rows * t, slice(side * half, (side + 1) * half))
                columns.append(jnp.concatenate([heat_ref[at], moist_ref[at]], axis=1))
    soundings = jnp.concatenate(columns, axis=0)
    for k, out_ref in enumerate(out_refs):
        target = []
        for place, base in slots:
            near = place - k * width
            target.append(jnp.where((near >= 0) & (near < width), base + near, -1.0))
        total = out_ref.shape[0]
        tile = min(256, total)
        for start in range(0, total, tile):
            slot = (lax.broadcasted_iota(i32, (tile, LANES), 0) + start).astype(f32)
            picks = jnp.concatenate(
                [
                    jnp.where(slot == one[m : m + 1], 1.0, 0.0).astype(bf16)
                    for one in target
                    for m in range(rows)
                ],
                axis=1,
            )
            out_ref[start : start + tile] = jnp.dot(
                picks, soundings, preferred_element_type=f32
            ).astype(bf16)


def plan_kernel(regimes, part, chunks, group_ref, label_ref, column_ref, pack_ref):
    labels = label_ref[...]
    half = labels.shape[1] // 2
    mine = group_ref[0]
    width = part // chunks
    sides = []
    for side in range(2):
        index = folded(labels, side * half, half)
        rank, member, count = ranked(index, regimes)
        sides.append((index.astype(f32), rank, member, jnp.maximum(count - part, 0.0)))
    own = [jnp.where(mine == 0, a, b) for a, b in zip(*sides)]
    other = [jnp.where(mine == 0, b, a) for a, b in zip(*sides)]
    lane = lax.broadcasted_iota(i32, (1, LANES), 1)
    for k in range(chunks):
        index, rank, member, spare = own
        spare = jnp.clip(spare - k * width, 0.0, width)
        offset = jnp.zeros((1, LANES), f32)
        at = jnp.zeros(rank.shape, f32)
        for r in range(regimes):
            at = at + member[r] * offset
            offset = offset + spare[r]
        near = part - 1.0 - rank - k * width
        kept = jnp.where((near >= 0) & (near < width), index * width + near, -1.0)
        near = rank - part - k * width
        come = jnp.where((near >= 0) & (near < width), at + near, -1.0)
        rows = rank.shape[0]
        column_ref[:, 2 * k * rows : (2 * k + 1) * rows] = kept.T
        column_ref[:, (2 * k + 1) * rows : (2 * k + 2) * rows] = come.T
        spare = jnp.clip(other[3] - k * width, 0.0, width)
        offset = jnp.zeros((1, LANES), f32)
        per_row = LANES // width
        for r in range(regimes):
            if r % per_row == 0:
                line = jnp.full((1, LANES), -1.0)
            near = (lane - (r % per_row) * width).astype(f32)
            line = jnp.where((near >= 0) & (near < spare[r]), offset + near, line)
            offset = offset + spare[r]
            if r % per_row == per_row - 1:
                pack_ref[k, r // per_row : r // per_row + 1] = line


def pack_kernel(pack_ref, result_ref, out_ref):
    room = out_ref.shape[0]
    slot = lax.broadcasted_iota(i32, (room, LANES), 0).astype(f32)
    picks = jnp.concatenate(
        [
            jnp.where(slot == pack_ref[m : m + 1], 1.0, 0.0).astype(bf16)
            for m in range(pack_ref.shape[0])
        ],
        axis=1,
    )
    out_ref[...] = jnp.dot(picks, result_ref[...], preferred_element_type=f32).astype(bf16)


def place_kernel(chunks, column_ref, *refs):
    sources = refs[: 2 * chunks]
    heat_ref, moist_ref = refs[2 * chunks :]
    half, levels = heat_ref.shape[1:]
    rows = heat_ref.shape[0] * half // LANES
    for m in range(rows):
        total = None
        for n, source in enumerate(sources):
            size = source.shape[0]
            slot = lax.broadcasted_iota(i32, (LANES, size), 1).astype(f32)
            wanted = column_ref[:, n * rows + m : n * rows + m + 1]
            picks = jnp.where(slot == wanted, 1.0, 0.0).astype(bf16)
            term = jnp.dot(picks, source[...], preferred_element_type=f32)
            total = term if total is None else total + term
        total = total.astype(bf16)
        for t in range(LANES // half):
            heat_ref[m + rows * t] = total[t * half : (t + 1) * half, :levels]
            moist_ref[m + rows * t] = total[t * half : (t + 1) * half, levels:]


def silu(s):
    h = 0.5 * s
    return h + h * jnp.tanh(h)


def network_kernel(x_ref, first_ref, second_ref, third_ref, last_ref, out_ref, one_ref, two_ref):
    def layer(source, weight, target):
        total = weight.shape[1]
        tile = min(256, total)
        for start in range(0, total, tile):
            sums = jnp.dot(
                source[...], weight[:, start : start + tile], preferred_element_type=f32
            )
            target[:, start : start + tile] = silu(sums).astype(bf16)

    layer(x_ref, first_ref, one_ref)
    layer(one_ref, second_ref, two_ref)
    layer(two_ref, third_ref, one_ref)
    out_ref[...] = jnp.dot(one_ref[...], last_ref[...], preferred_element_type=f32).astype(bf16)


def network(x, first, second, third, last):
    rows, hidden = x.shape[0], first.shape[1]
    size = first.size + second.size + third.size + last.size
    return pl.pallas_call(
        network_kernel,
        out_shape=jax.ShapeDtypeStruct((rows, last.shape[1]), bf16),
        scratch_shapes=[pltpu.VMEM((rows, hidden), bf16)] * 2,
        compiler_params=params(24),
        cost_estimate=cost(2 * rows * size, 2 * size),
        name="network",
    )(x, first, second, third, last)


def dynamics_kernel(
    group_ref, rate_ref, e_in, n_in, p_in, left_ref, right_ref, e_out, n_out, p_out, e_ref, n_ref, p_ref
):
    deep, half = e_out.shape[:2]
    span = e_ref.shape[1]
    reach = span - half
    wide = e_in.shape[1]
    mine = group_ref[0]
    coef = rate_ref[...] * 0.5

    def block(ref, i):
        row = ref[i].astype(f32)
        return jnp.where(mine == 0, row[:span], row[wide - span :])

    edge = jnp.zeros((8,) + (LANES,), f32)

    for ref in (n_ref, p_ref):

        def clear(i, _, ref=ref):
            ref[i, 0:8] = edge
            ref[i, 8 + span : 16 + span] = edge
            return 0

        lax.fori_loop(0, ref.shape[0], clear, 0)

    start = 0
    for source, ref, off, width in (
        (p_in, p_ref, 8, reach),
        (e_in, e_ref, 0, reach - 1),
        (n_in, n_ref, 8, reach - 2),
    ):
        rows = slice(off, off + span)

        def load(i, _, source=source, ref=ref, rows=rows, width=width):
            ref[i + width, rows] = block(source, i)
            return 0

        lax.fori_loop(0, deep, load, 0)

        def load_sides(i, _, ref=ref, rows=rows, width=width, start=start):
            ref[i, rows] = left_ref[start + i].astype(f32)
            ref[i + width + deep, rows] = right_ref[start + i].astype(f32)
            return 0

        lax.fori_loop(0, width, load_sides, 0)
        start += width

    mid, low, high = slice(8, 8 + span), slice(7, 7 + span), slice(9, 9 + span)
    for s in range(SUB):
        done = 2 * s

        def winds(i, _):
            e_ref[i] = e_ref[i] - coef * (p_ref[i + 2, mid] - p_ref[i, mid])
            return 0

        lax.fori_loop(done, e_ref.shape[0] - done, winds, 0)

        def north(i, _):
            n_ref[i, mid] = n_ref[i, mid] - coef * (p_ref[i + 2, high] - p_ref[i + 2, low])
            return 0

        lax.fori_loop(done, n_ref.shape[0] - done, north, 0)

        def pressure(i, _):
            p_ref[i + 2, mid] = p_ref[i + 2, mid] - coef * (
                (e_ref[i + 2] - e_ref[i]) + (n_ref[i, high] - n_ref[i, low])
            )
            return 0

        lax.fori_loop(done, n_ref.shape[0] - done, pressure, 0)

    for ref, out, off, width in (
        (e_ref, e_out, 0, reach - 1),
        (n_ref, n_out, 8, reach - 2),
        (p_ref, p_out, 8, reach),
    ):

        def store(i, _, ref=ref, out=out, off=off, width=width):
            near = ref[i + width, off : off + half]
            far = ref[i + width, off + reach : off + reach + half]
            out[i] = jnp.where(mine == 0, near, far).astype(bf16)
            return 0

        lax.fori_loop(0, deep, store, 0)


def dynamics(group, rate, e, n, p, left, right):
    deep, wide, levels = e.shape
    half = wide // 2
    reach = 2 * SUB
    span = half + reach
    out = jax.ShapeDtypeStruct((deep, half, levels), bf16)
    cells = deep * half * levels
    return pl.pallas_call(
        dynamics_kernel,
        out_shape=(out,) * 3,
        in_specs=[pl.BlockSpec(memory_space=pltpu.SMEM)] + [pl.BlockSpec(memory_space=pltpu.VMEM)] * 6,
        scratch_shapes=[
            pltpu.VMEM((deep + 2 * (reach - 1), span, levels), f32),
            pltpu.VMEM((deep + 2 * (reach - 2), span + 16, levels), f32),
            pltpu.VMEM((deep + 2 * reach, span + 16, levels), f32),
        ],
        compiler_params=params(16),
        cost_estimate=cost(cells * 200, cells * 24),
        name="dynamics",
    )(group, rate, e, n, p, left, right)


def halos(e, n, p, mine):
    wide = e.shape[1]
    half, reach = wide // 2, 2 * SUB
    span = half + reach
    count = lax.axis_size("blk")
    cut = lambda f: lax.dynamic_slice_in_dim(f, mine * (wide - span), span, 1)
    widths = ((p, reach), (e, reach - 1), (n, reach - 2))
    tail = cut(jnp.concatenate([f[f.shape[0] - w :] for f, w in widths], axis=0))
    head = cut(jnp.concatenate([f[:w] for f, w in widths], axis=0))
    left = lax.ppermute(tail, "blk", [(i, (i + 1) % count) for i in range(count)])
    right = lax.ppermute(head, "blk", [((i + 1) % count, i) for i in range(count)])
    return left, right


def room_for(chunk, width, part, regimes):
    most = 0
    for above in range(regimes):
        short = part * (regimes - above) - above * chunk * width
        most = max(most, min(above * width, short))
    return -(-most // 16) * 16


def local(
    zonal_velocity_field,
    meridional_velocity_field,
    barometric_disturbance,
    delayed_thermal_deviation,
    delayed_moisture_deviation,
    flow_category_label,
    advective_stability_number,
    initial_dense_matrix,
    middle_dense_matrix,
    closing_dense_matrix,
    final_readout_matrix,
):
    mine = lax.axis_index("grp")
    group = jnp.full((1,), mine, i32)
    regimes = lax.axis_size("blk")
    deep, wide, levels = zonal_velocity_field.shape
    half = wide // 2
    profile = 2 * levels
    part = deep * wide // regimes // 2
    chunks = CHUNKS
    width = part // chunks
    size = regimes * width
    rows = deep * half // LANES
    smem = pl.BlockSpec(memory_space=pltpu.SMEM)
    vmem = pl.BlockSpec(memory_space=pltpu.VMEM)

    left, right = halos(
        zonal_velocity_field, meridional_velocity_field, barometric_disturbance, mine
    )
    outgoing = pl.pallas_call(
        functools.partial(route_kernel, regimes, part),
        out_shape=(jax.ShapeDtypeStruct((size, profile), bf16),) * chunks,
        in_specs=[smem, vmem, vmem, vmem],
        compiler_params=params(24),
        cost_estimate=cost(2 * regimes * part * deep * wide * profile, 2 * MIB),
        name="route",
    )(group, flow_category_label, delayed_thermal_deviation, delayed_moisture_deviation)
    column_plan, pack_plan = pl.pallas_call(
        functools.partial(plan_kernel, regimes, part, chunks),
        out_shape=(
            jax.ShapeDtypeStruct((LANES, 2 * chunks * rows), f32),
            jax.ShapeDtypeStruct((chunks, size // LANES, LANES), f32),
        ),
        in_specs=[smem, vmem],
        compiler_params=params(16),
        cost_estimate=cost(MIB, MIB),
        name="plan",
    )(group, flow_category_label)

    arrived = [
        lax.all_to_all(
            one.reshape(regimes, width, profile), "blk", split_axis=0, concat_axis=0, tiled=True
        )
        for one in outgoing
    ]
    returned = [
        lax.all_to_all(
            network(
                one.reshape(size, profile),
                initial_dense_matrix[0],
                middle_dense_matrix[0],
                closing_dense_matrix[0],
                final_readout_matrix[0],
            ).reshape(regimes, width, profile),
            "blk",
            split_axis=0,
            concat_axis=0,
            tiled=True,
        ).reshape(size, profile)
        for one in arrived
    ]
    sources = []
    for k, one in enumerate(returned):
        room = room_for(k, width, part, regimes)
        packed = pl.pallas_call(
            pack_kernel,
            out_shape=jax.ShapeDtypeStruct((room, profile), bf16),
            compiler_params=params(16),
            cost_estimate=cost(2 * room * size * profile, MIB),
            name="pack",
        )(pack_plan[k], one)
        sources += [one, lax.ppermute(packed, "grp", [(0, 1), (1, 0)])]
    out = jax.ShapeDtypeStruct((deep, half, levels), bf16)
    heating, moistening = pl.pallas_call(
        functools.partial(place_kernel, chunks),
        out_shape=(out, out),
        compiler_params=params(24),
        cost_estimate=cost(2 * deep * half * sum(s.shape[0] for s in sources) * profile, 2 * MIB),
        name="place",
    )(column_plan, *sources)
    east, north, pressure = dynamics(
        group,
        advective_stability_number.reshape(1, levels),
        zonal_velocity_field,
        meridional_velocity_field,
        barometric_disturbance,
        left,
        right,
    )
    return east, north, pressure, heating, moistening


def solution(mesh):
    return jax.shard_map(
        local,
        mesh=mesh,
        in_specs=(P("blk", None, None),) * 5
        + (P("blk", None), P())
        + (P("blk", None, None),) * 4,
        out_specs=(P("blk", "grp", None),) * 5,
        check_vma=False,
    )
```

```python
import functools
import jax
import jax.numpy as jnp
from jax import lax
from jax.experimental import pallas as pl
from jax.experimental.pallas import tpu as pltpu
from jax.sharding import PartitionSpec as P

SUB = 4
ROOM = 128
LANES = 128
MIB = 1 << 20
bf16, f32, i32 = jnp.bfloat16, jnp.float32, jnp.int32
SMEM = pl.BlockSpec(memory_space=pltpu.SMEM)
VMEM = pl.BlockSpec(memory_space=pltpu.VMEM)
HBM = pl.BlockSpec(memory_space=pltpu.HBM)
ANY = pl.BlockSpec(memory_space=pl.ANY)


def params(mib):
    return pltpu.CompilerParams(vmem_limit_bytes=mib * MIB)


TOKEN = jax.ShapeDtypeStruct((8, LANES), f32)


def in_hbm(*arrays):
    return [pltpu.with_memory_space_constraint(x, pltpu.HBM) for x in arrays]


def cost(flops, moved):
    return pl.CostEstimate(flops=flops, bytes_accessed=moved, transcendentals=0)


def folded(labels, start, half):
    rows = labels.shape[0] * half // LANES
    side = labels[:, start : start + half]
    return jnp.concatenate(
        [side[t * rows : (t + 1) * rows] for t in range(LANES // half)], axis=1
    )


def ranked(labels, regimes):
    rows = labels.shape[0]
    shape = (regimes, rows, LANES)
    member = jnp.where(
        lax.broadcasted_iota(i32, shape, 0) == jnp.broadcast_to(labels[None], shape), 1.0, 0.0
    )
    flat = member.reshape(regimes * rows, LANES).astype(bf16)
    first = lax.broadcasted_iota(i32, (LANES, LANES), 0)
    second = lax.broadcasted_iota(i32, (LANES, LANES), 1)
    earlier = jnp.where(first < second, 1.0, 0.0).astype(bf16)
    within = jnp.dot(flat, earlier, preferred_element_type=f32).reshape(shape)
    totals = jnp.dot(
        flat, jnp.ones((LANES, LANES), bf16), preferred_element_type=f32
    ).reshape(shape)
    before = jnp.zeros((regimes, 1, LANES), f32)
    rank = jnp.zeros((rows, LANES), f32)
    row_ranks = []
    for m in range(rows):
        row_ranks.append(
            jnp.sum(member[:, m : m + 1] * (within[:, m : m + 1] + before), axis=0)
        )
        before = before + totals[:, m : m + 1]
    rank = jnp.concatenate(row_ranks, axis=0)
    return rank, member, before


def route_kernel(
    regimes, part, group_ref, label_in, heat_in, moist_in, out_ref, token_ref, label_ref, heat_ref, moist_ref, sem
):
    token_ref[...] = jnp.zeros_like(token_ref)
    deep, wide, levels = heat_ref.shape
    half = wide // 2
    rows = deep * half // LANES
    pieces = LANES // half
    first = pltpu.make_async_copy(label_in, label_ref, sem.at[0])
    first.start()
    copies = []
    for t in range(pieces):
        at = slice(t * rows, (t + 1) * rows)
        for source, target in ((heat_in, heat_ref), (moist_in, moist_ref)):
            n = len(copies) + 1
            copies.append(pltpu.make_async_copy(source.at[at], target.at[at], sem.at[n]))
            copies[-1].start()
    mine = group_ref[0]
    first.wait()
    labels = label_ref[...]
    targets = []
    for side in range(2):
        index = folded(labels, side * half, half)
        rank, _, _ = ranked(index, regimes)
        place = jnp.where(mine == side, part - 1.0 - rank, rank - part)
        targets.append(jnp.where(place >= 0, index.astype(f32) * part + place, -1.0))
    target = jnp.concatenate(targets, axis=0)
    for copy in copies:
        copy.wait()
    columns = []
    for side in range(2):
        for m in range(rows):
            for t in range(pieces):
                at = (m + rows * t, slice(side * half, (side + 1) * half))
                columns.append(jnp.concatenate([heat_ref[at], moist_ref[at]], axis=1))
    soundings = jnp.concatenate(columns, axis=0)
    total = out_ref.shape[0]
    tile = min(256, total)
    for start in range(0, total, tile):
        slot = (lax.broadcasted_iota(i32, (tile, LANES), 0) + start).astype(f32)
        picks = jnp.concatenate(
            [jnp.where(slot == target[m : m + 1], 1.0, 0.0).astype(bf16) for m in range(2 * rows)],
            axis=1,
        )
        out_ref[start : start + tile] = jnp.dot(
            picks, soundings, preferred_element_type=f32
        ).astype(bf16)


def plan_kernel(regimes, part, group_ref, label_ref, _, column_ref, pack_ref, crowd_ref):
    labels = label_ref[...]
    half = labels.shape[1] // 2
    mine = group_ref[0]
    sides = []
    for side in range(2):
        index = folded(labels, side * half, half)
        rank, member, count = ranked(index, regimes)
        sides.append((index.astype(f32), rank, member, jnp.maximum(count - part, 0.0)))
    index, rank, member, spare = [jnp.where(mine == 0, a, b) for a, b in zip(*sides)]
    rows = rank.shape[0]
    offset = jnp.zeros((1, LANES), f32)
    at = jnp.zeros(rank.shape, f32)
    for r in range(regimes):
        at = at + member[r] * offset
        offset = offset + spare[r]
    crowd_ref[0] = (jnp.max(offset) > ROOM).astype(i32)
    kept = jnp.where(rank < part, index * part + (part - 1.0 - rank), -1.0)
    come = jnp.where(rank >= part, at + (rank - part), -1.0)
    column_ref[:, :rows] = kept.T
    column_ref[:, rows : 2 * rows] = come.T
    spare = jnp.where(mine == 0, sides[1][3], sides[0][3])
    lane = lax.broadcasted_iota(i32, (1, LANES), 1)
    offset = jnp.zeros((1, LANES), f32)
    per_row = LANES // part
    for r in range(regimes):
        if r % per_row == 0:
            line = jnp.full((1, LANES), -1.0)
        near = (lane - (r % per_row) * part).astype(f32)
        line = jnp.where((near >= 0) & (near < spare[r]), offset + near, line)
        offset = offset + spare[r]
        if r % per_row == per_row - 1:
            pack_ref[r // per_row : r // per_row + 1] = line


def plan(regimes, part, rows, group, labels, after):
    return pl.pallas_call(
        functools.partial(plan_kernel, regimes, part),
        out_shape=(
            jax.ShapeDtypeStruct((LANES, 2 * rows), f32),
            jax.ShapeDtypeStruct((regimes * part // LANES, LANES), f32),
            jax.ShapeDtypeStruct((1,), i32),
        ),
        in_specs=[SMEM, VMEM, VMEM],
        out_specs=(VMEM, VMEM, SMEM),
        compiler_params=params(12),
        cost_estimate=cost(MIB, MIB),
        name="plan",
    )(group, labels, after)


def pack_kernel(pack_ref, result_ref, _, out_ref):
    slot = lax.broadcasted_iota(i32, (out_ref.shape[0], LANES), 0).astype(f32)
    picks = jnp.concatenate(
        [
            jnp.where(slot == pack_ref[m : m + 1], 1.0, 0.0).astype(bf16)
            for m in range(pack_ref.shape[0])
        ],
        axis=1,
    )
    out_ref[...] = jnp.dot(picks, result_ref[...], preferred_element_type=f32).astype(bf16)


def pack(room, pack_plan, result, after):
    return pl.pallas_call(
        pack_kernel,
        out_shape=jax.ShapeDtypeStruct((room, result.shape[1]), bf16),
        in_specs=[VMEM, VMEM, VMEM],
        compiler_params=params(12),
        cost_estimate=cost(2 * room * result.size, MIB),
        name="pack",
    )(pack_plan, result, after)


def picked(wanted, source_ref):
    slot = lax.broadcasted_iota(i32, (LANES, source_ref.shape[0]), 1).astype(f32)
    picks = jnp.where(slot == wanted, 1.0, 0.0).astype(bf16)
    return jnp.dot(picks, source_ref[...], preferred_element_type=f32)


def keep_kernel(column_ref, result_ref, packed_ref, out_ref):
    del packed_ref
    for m in range(column_ref.shape[1] // 2):
        out_ref[m * LANES : (m + 1) * LANES] = picked(
            column_ref[:, m : m + 1], result_ref
        ).astype(bf16)


def place_kernel(column_ref, kept_ref, come_ref, heat_ref, moist_ref):
    half, levels = heat_ref.shape[1:]
    rows = heat_ref.shape[0] * half // LANES
    for m in range(rows):
        total = picked(column_ref[:, rows + m : rows + m + 1], come_ref)
        total = (total + kept_ref[m * LANES : (m + 1) * LANES].astype(f32)).astype(bf16)
        for t in range(LANES // half):
            heat_ref[m + rows * t] = total[t * half : (t + 1) * half, :levels]
            moist_ref[m + rows * t] = total[t * half : (t + 1) * half, levels:]


def placed(room, shape, column_plan, pack_plan, result, after):
    packed = pack(room, pack_plan, result, after)
    come = lax.ppermute(packed, "grp", [(0, 1), (1, 0)])
    kept = pl.pallas_call(
        keep_kernel,
        out_shape=jax.ShapeDtypeStruct((shape[0] * shape[1], result.shape[1]), bf16),
        in_specs=[VMEM, VMEM, HBM],
        compiler_params=params(12),
        cost_estimate=cost(2 * shape[0] * shape[1] * result.size, MIB),
        name="keep",
    )(column_plan, result, packed)
    out = jax.ShapeDtypeStruct(shape, bf16)
    return tuple(
        pl.pallas_call(
            place_kernel,
            out_shape=(out, out),
            compiler_params=params(12),
            cost_estimate=cost(2 * shape[0] * shape[1] * come.size, 2 * MIB),
            name="place",
        )(column_plan, kept, come)
    )


def silu(s):
    h = 0.5 * s
    return h + h * jnp.tanh(h)


def layer(source, weight, target):
    total = weight.shape[1]
    tile = min(256, total)
    for i in range(total // tile):
        at = slice(i * tile, (i + 1) * tile)
        sums = jnp.dot(source[...], weight[:, at], preferred_element_type=f32)
        target[:, at] = silu(sums).astype(bf16)


def front_kernel(x_ref, first_in, second_in, out_ref, one_ref, first_ref, second_ref, sem):
    first = pltpu.make_async_copy(first_in.at[0], first_ref, sem.at[0])
    second = pltpu.make_async_copy(second_in.at[0], second_ref, sem.at[1])
    first.start()
    second.start()
    first.wait()
    layer(x_ref, first_ref, one_ref)
    second.wait()
    layer(one_ref, second_ref, out_ref)


def back_kernel(two_ref, third_ref, last_ref, _, __, out_ref, token_ref, three_ref):
    token_ref[...] = jnp.zeros_like(token_ref)
    layer(two_ref, third_ref, three_ref)
    out_ref[...] = jnp.dot(three_ref[...], last_ref[...], preferred_element_type=f32).astype(bf16)


def front(x, first, second):
    rows, hidden = x.shape[0], first.shape[2]
    size = first.size + second.size
    return pl.pallas_call(
        front_kernel,
        out_shape=jax.ShapeDtypeStruct((rows, hidden), bf16),
        in_specs=[VMEM] + [HBM] * 2,
        scratch_shapes=[pltpu.VMEM((rows, hidden), bf16)]
        + [pltpu.VMEM(w.shape[1:], bf16) for w in (first, second)]
        + [pltpu.SemaphoreType.DMA((2,))],
        compiler_params=params(14),
        cost_estimate=cost(2 * rows * size, 2 * size),
        name="front",
    )(x, *in_hbm(first, second))


def back(two, third, last, *after):
    rows, hidden = two.shape
    size = third.size + last.size
    return pl.pallas_call(
        back_kernel,
        out_shape=(jax.ShapeDtypeStruct((rows, last.shape[1]), bf16), TOKEN),
        in_specs=[VMEM] * 3 + [ANY] * len(after),
        scratch_shapes=[pltpu.VMEM((rows, hidden), bf16)],
        compiler_params=params(14),
        cost_estimate=cost(2 * rows * size, 2 * size),
        name="back",
    )(two, third, last, *after)


def dynamics_kernel(
    group_ref, rate_ref, e_in, n_in, p_in, left_in, right_in, _, e_out, n_out, p_out, token_ref,
    e_ref, n_ref, p_ref, left_ref, right_ref, sem,
):
    sides = [
        pltpu.make_async_copy(left_in, left_ref, sem.at[0]),
        pltpu.make_async_copy(right_in, right_ref, sem.at[1]),
    ]
    for side in sides:
        side.start()
    token_ref[...] = jnp.zeros_like(token_ref)
    deep, half = e_out.shape[:2]
    span = e_ref.shape[1]
    reach = span - half
    wide = e_in.shape[1]
    mine = group_ref[0]
    coef = rate_ref[...] * 0.5

    edge = jnp.zeros((8, LANES), f32)

    for ref in (n_ref, p_ref):

        def clear(i, _, ref=ref):
            ref[i, 0:8] = edge
            ref[i, 8 + span : 16 + span] = edge
            return 0

        lax.fori_loop(0, ref.shape[0], clear, 0)

    fields = (
        (p_in, p_out, p_ref, 8, reach),
        (e_in, e_out, e_ref, 0, reach - 1),
        (n_in, n_out, n_ref, 8, reach - 2),
    )

    def load(i, _):
        for source, _, ref, off, width in fields:
            row = source[i].astype(f32)
            ref[i + width, off : off + span] = jnp.where(
                mine == 0, row[:span], row[wide - span :]
            )
        return 0

    lax.fori_loop(0, deep, load, 0)
    for side in sides:
        side.wait()
    start = 0
    for _, _, ref, off, width in fields:
        for i in range(width):
            ref[i, off : off + span] = left_ref[start + i].astype(f32)
            ref[i + width + deep, off : off + span] = right_ref[start + i].astype(f32)
        start += width

    mid, low, high = slice(8, 8 + span), slice(7, 7 + span), slice(9, 9 + span)

    def wind(i):
        e_ref[i] = e_ref[i] - coef * (p_ref[i + 2, mid] - p_ref[i, mid])

    for s in range(SUB):
        first, last = 2 * s, n_ref.shape[0] - 2 * s
        wind(first)

        def winds(k, _, first=first):
            for i in (first + 2 * k, first + 2 * k + 1):
                wind(i + 1)
                n_ref[i, mid] = n_ref[i, mid] - coef * (p_ref[i + 2, high] - p_ref[i + 2, low])
            return 0

        lax.fori_loop(0, (last - first) // 2, winds, 0)
        wind(last + 1)

        def pressure(k, _, first=first):
            for i in (first + 2 * k, first + 2 * k + 1):
                p_ref[i + 2, mid] = p_ref[i + 2, mid] - coef * (
                    (e_ref[i + 2] - e_ref[i]) + (n_ref[i, high] - n_ref[i, low])
                )
            return 0

        lax.fori_loop(0, (last - first) // 2, pressure, 0)

    def store(i, _):
        for _, out, ref, off, width in fields:
            near = ref[i + width, off : off + half]
            far = ref[i + width, off + reach : off + reach + half]
            out[i] = jnp.where(mine == 0, near, far).astype(bf16)
        return 0

    lax.fori_loop(0, deep, store, 0)


def dynamics(group, rate, e, n, p, left, right, after):
    deep, wide, levels = e.shape
    half = wide // 2
    reach = 2 * SUB
    span = half + reach
    out = jax.ShapeDtypeStruct((deep, half, levels), bf16)
    cells = deep * half * levels
    return pl.pallas_call(
        dynamics_kernel,
        out_shape=(out,) * 3 + (TOKEN,),
        in_specs=[SMEM] + [VMEM] * 4 + [ANY] * 2 + [VMEM],
        scratch_shapes=[
            pltpu.VMEM((deep + 2 * (reach - 1), span, levels), f32),
            pltpu.VMEM((deep + 2 * (reach - 2), span + 16, levels), f32),
            pltpu.VMEM((deep + 2 * reach, span + 16, levels), f32),
            pltpu.VMEM(left.shape, bf16),
            pltpu.VMEM(right.shape, bf16),
            pltpu.SemaphoreType.DMA((2,)),
        ],
        compiler_params=params(12),
        cost_estimate=cost(cells * 200, cells * 24),
        name="dynamics",
    )(group, rate, e, n, p, left, right, after)


def edges_kernel(group_ref, e_ref, n_ref, p_ref, _, tail_ref, head_ref):
    deep, wide = e_ref.shape[:2]
    span = tail_ref.shape[1]
    mine = group_ref[0]
    reach = 2 * SUB
    at = 0
    for ref, width in ((p_ref, reach), (e_ref, reach - 1), (n_ref, reach - 2)):
        for i in range(width):
            for out, row in ((tail_ref, deep - width + i), (head_ref, i)):
                whole = ref[row].astype(f32)
                out[at + i] = jnp.where(mine == 0, whole[:span], whole[wide - span :]).astype(bf16)
        at += width


def halos(group, e, n, p, after):
    wide, levels = e.shape[1:]
    reach = 2 * SUB
    count = lax.axis_size("blk")
    out = jax.ShapeDtypeStruct((3 * reach - 3, wide // 2 + reach, levels), bf16)
    tail, head = pl.pallas_call(
        edges_kernel,
        out_shape=(out, out),
        in_specs=[SMEM] + [VMEM] * 4,
        compiler_params=params(12),
        cost_estimate=cost(MIB, 2 * MIB),
        name="edges",
    )(group, e, n, p, after)
    left = lax.ppermute(tail, "blk", [(i, (i + 1) % count) for i in range(count)])
    right = lax.ppermute(head, "blk", [((i + 1) % count, i) for i in range(count)])
    return left, right


def local(
    zonal_velocity_field,
    meridional_velocity_field,
    barometric_disturbance,
    delayed_thermal_deviation,
    delayed_moisture_deviation,
    flow_category_label,
    advective_stability_number,
    initial_dense_matrix,
    middle_dense_matrix,
    closing_dense_matrix,
    final_readout_matrix,
):
    group = jnp.full((1,), lax.axis_index("grp"), i32)
    regimes = lax.axis_size("blk")
    deep, wide, levels = zonal_velocity_field.shape
    half = wide // 2
    profile = 2 * levels
    part = deep * wide // regimes // 2
    size = regimes * part
    rows = deep * half // LANES

    def swapped(one):
        one = one.reshape(regimes, part, profile)
        one = lax.all_to_all(one, "blk", split_axis=0, concat_axis=0, tiled=True)
        return one.reshape(size, profile)

    sent, routed = pl.pallas_call(
        functools.partial(route_kernel, regimes, part),
        out_shape=(jax.ShapeDtypeStruct((size, profile), bf16), TOKEN),
        in_specs=[SMEM, HBM, HBM, HBM],
        scratch_shapes=[
            pltpu.VMEM((deep, wide), i32),
            pltpu.VMEM((deep, wide, levels), bf16),
            pltpu.VMEM((deep, wide, levels), bf16),
            pltpu.SemaphoreType.DMA((1 + 2 * (LANES // half),)),
        ],
        compiler_params=params(16),
        cost_estimate=cost(2 * size * deep * wide * profile, 2 * MIB),
        name="route",
    )(
        group,
        *in_hbm(flow_category_label, delayed_thermal_deviation, delayed_moisture_deviation),
    )
    arrived = swapped(sent)
    left, right = halos(
        group, zonal_velocity_field, meridional_velocity_field, barometric_disturbance, routed
    )
    column_plan, pack_plan, crowded = plan(regimes, part, rows, group, flow_category_label, routed)
    two = front(arrived, initial_dense_matrix, middle_dense_matrix)
    result, worked = back(two, closing_dense_matrix[0], final_readout_matrix[0], left, right)
    returned = swapped(result)
    east, north, pressure, moved = dynamics(
        group,
        advective_stability_number.reshape(1, levels),
        zonal_velocity_field,
        meridional_velocity_field,
        barometric_disturbance,
        left,
        right,
        worked,
    )
    shape = (deep, half, levels)
    heating, moistening = lax.cond(
        crowded[0] > 0,
        functools.partial(placed, size // 2, shape),
        functools.partial(placed, min(ROOM, size // 2), shape),
        column_plan,
        pack_plan,
        returned,
        moved,
    )
    return east, north, pressure, heating, moistening


def solution(mesh):
    return jax.shard_map(
        local,
        mesh=mesh,
        in_specs=(P("blk", None, None),) * 5
        + (P("blk", None), P())
        + (P("blk", None, None),) * 4,
        out_specs=(P("blk", "grp", None),) * 5,
        check_vma=False,
    )
```

```python
import functools
import jax
import jax.numpy as jnp
from jax import lax
from jax.experimental import pallas as pl
from jax.experimental.pallas import tpu as pltpu
from jax.sharding import PartitionSpec as P

SUB = 4
BATCHES = 2
ROOM = 80
LANES = 128
MIB = 1 << 20
bf16, f32, i32 = jnp.bfloat16, jnp.float32, jnp.int32
SMEM = pl.BlockSpec(memory_space=pltpu.SMEM)
VMEM = pl.BlockSpec(memory_space=pltpu.VMEM)
HBM = pl.BlockSpec(memory_space=pltpu.HBM)
ANY = pl.BlockSpec(memory_space=pl.ANY)


def params(mib):
    return pltpu.CompilerParams(vmem_limit_bytes=mib * MIB)


TOKEN = jax.ShapeDtypeStruct((8, LANES), f32)


def in_hbm(*arrays):
    return [pltpu.with_memory_space_constraint(x, pltpu.HBM) for x in arrays]


def cost(flops, moved):
    return pl.CostEstimate(flops=flops, bytes_accessed=moved, transcendentals=0)


def folded(labels, start, half):
    rows = labels.shape[0] * half // LANES
    side = labels[:, start : start + half]
    return jnp.concatenate(
        [side[t * rows : (t + 1) * rows] for t in range(LANES // half)], axis=1
    )


def ranked(labels, regimes):
    rows = labels.shape[0]
    shape = (regimes, rows, LANES)
    member = jnp.where(
        lax.broadcasted_iota(i32, shape, 0) == jnp.broadcast_to(labels[None], shape), 1.0, 0.0
    )
    flat = member.reshape(regimes * rows, LANES).astype(bf16)
    first = lax.broadcasted_iota(i32, (LANES, LANES), 0)
    second = lax.broadcasted_iota(i32, (LANES, LANES), 1)
    earlier = jnp.where(first < second, 1.0, 0.0).astype(bf16)
    totals = jnp.dot(flat, jnp.ones((LANES, LANES), bf16), preferred_element_type=f32)
    within = jnp.dot(flat, earlier, preferred_element_type=f32)
    totals = totals.reshape(shape)
    row = lax.broadcasted_iota(i32, (1, rows, LANES), 1)
    before, step = totals, 1
    while step < rows:
        before = before + jnp.where(row >= step, pltpu.roll(before, step, 1), 0.0)
        step *= 2
    count = before[:, rows - 1 :]
    rank = jnp.sum(member * (within.reshape(shape) + (before - totals)), axis=0)
    return rank, member, count


def route_kernel(
    regimes, part, group_ref, label_in, heat_in, moist_in, out_ref, token_ref, label_ref, heat_ref, moist_ref, sem
):
    token_ref[...] = jnp.zeros_like(token_ref)
    deep, wide, levels = heat_ref.shape
    half = wide // 2
    rows = deep * half // LANES
    pieces = LANES // half
    first = pltpu.make_async_copy(label_in, label_ref, sem.at[0])
    first.start()
    copies = []
    for t in range(pieces):
        at = slice(t * rows, (t + 1) * rows)
        for source, target in ((heat_in, heat_ref), (moist_in, moist_ref)):
            n = len(copies) + 1
            copies.append(pltpu.make_async_copy(source.at[at], target.at[at], sem.at[n]))
            copies[-1].start()
    mine = group_ref[0]
    first.wait()
    labels = label_ref[...]
    targets = []
    for side in range(2):
        index = folded(labels, side * half, half)
        rank, _, _ = ranked(index, regimes)
        place = jnp.where(mine == side, part - 1.0 - rank, rank - part)
        targets.append(jnp.where(place >= 0, index.astype(f32) * part + place, -1.0))
    target = jnp.concatenate(targets, axis=0)
    for copy in copies:
        copy.wait()
    columns = []
    for side in range(2):
        for m in range(rows):
            for t in range(pieces):
                at = (m + rows * t, slice(side * half, (side + 1) * half))
                columns.append(jnp.concatenate([heat_ref[at], moist_ref[at]], axis=1))
    soundings = jnp.concatenate(columns, axis=0)
    total = out_ref.shape[0]
    tile = min(256, total)
    slot = lax.broadcasted_iota(i32, (tile, LANES), 0).astype(f32).astype(bf16)
    yes, no = jnp.ones((), bf16), jnp.zeros((), bf16)
    for start in range(0, total, tile):
        near = target - start
        near = jnp.where((near >= 0) & (near < tile), near, -1.0).astype(bf16)
        picks = jnp.concatenate(
            [jnp.where(slot == near[m : m + 1], yes, no) for m in range(2 * rows)], axis=1
        )
        out_ref[start : start + tile] = jnp.dot(
            picks, soundings, preferred_element_type=f32
        ).astype(bf16)


def plan_kernel(regimes, part, group_ref, label_ref, _, column_ref, pack_ref, crowd_ref):
    labels = label_ref[...]
    half = labels.shape[1] // 2
    mine = group_ref[0]
    sides = []
    for side in range(2):
        index = folded(labels, side * half, half)
        rank, member, count = ranked(index, regimes)
        sides.append((index.astype(f32), rank, member, jnp.maximum(count - part, 0.0)))
    index, rank, member, spare = [jnp.where(mine == 0, a, b) for a, b in zip(*sides)]
    rows = rank.shape[0]
    offset = jnp.zeros((1, LANES), f32)
    at = jnp.zeros(rank.shape, f32)
    for r in range(regimes):
        at = at + member[r] * offset
        offset = offset + spare[r]
    crowd_ref[0] = (jnp.max(offset) > ROOM).astype(i32)
    kept = jnp.where(rank < part, index * part + (part - 1.0 - rank), -1.0)
    come = jnp.where(rank >= part, at + (rank - part), -1.0)
    column_ref[:, :rows] = kept.T
    column_ref[:, rows : 2 * rows] = come.T
    spare = jnp.where(mine == 0, sides[1][3], sides[0][3])
    lane = lax.broadcasted_iota(i32, (1, LANES), 1)
    offset = jnp.zeros((1, LANES), f32)
    per_row = LANES // part
    for r in range(regimes):
        if r % per_row == 0:
            line = jnp.full((1, LANES), -1.0)
        near = (lane - (r % per_row) * part).astype(f32)
        line = jnp.where((near >= 0) & (near < spare[r]), offset + near, line)
        offset = offset + spare[r]
        if r % per_row == per_row - 1:
            pack_ref[r // per_row : r // per_row + 1] = line


def plan(regimes, part, rows, group, labels, after):
    return pl.pallas_call(
        functools.partial(plan_kernel, regimes, part),
        out_shape=(
            jax.ShapeDtypeStruct((LANES, 2 * rows), f32),
            jax.ShapeDtypeStruct((regimes * part // LANES, LANES), f32),
            jax.ShapeDtypeStruct((1,), i32),
        ),
        in_specs=[SMEM, VMEM, VMEM],
        out_specs=(VMEM, VMEM, SMEM),
        compiler_params=params(12),
        cost_estimate=cost(MIB, MIB),
        name="plan",
    )(group, labels, after)


def pack_kernel(pack_ref, result_ref, _, out_ref):
    slot = lax.broadcasted_iota(i32, (out_ref.shape[0], LANES), 0).astype(f32)
    picks = jnp.concatenate(
        [
            jnp.where(slot == pack_ref[m : m + 1], 1.0, 0.0).astype(bf16)
            for m in range(pack_ref.shape[0])
        ],
        axis=1,
    )
    out_ref[...] = jnp.dot(picks, result_ref[...], preferred_element_type=f32).astype(bf16)


def pack(room, pack_plan, result, after):
    return pl.pallas_call(
        pack_kernel,
        out_shape=jax.ShapeDtypeStruct((room, result.shape[1]), bf16),
        in_specs=[VMEM, VMEM, VMEM],
        compiler_params=params(12),
        cost_estimate=cost(2 * room * result.size, MIB),
        name="pack",
    )(pack_plan, result, after)


def picked(wanted, source_ref):
    slot = lax.broadcasted_iota(i32, (LANES, source_ref.shape[0]), 1).astype(f32)
    picks = jnp.where(slot == wanted, 1.0, 0.0).astype(bf16)
    return jnp.dot(picks, source_ref[...], preferred_element_type=f32)


def keep_kernel(column_ref, result_ref, packed_ref, out_ref):
    del packed_ref
    for m in range(column_ref.shape[1] // 2):
        out_ref[m * LANES : (m + 1) * LANES] = picked(
            column_ref[:, m : m + 1], result_ref
        ).astype(bf16)


def place_kernel(column_ref, kept_ref, come_ref, heat_ref, moist_ref):
    half, levels = heat_ref.shape[1:]
    rows = heat_ref.shape[0] * half // LANES
    for m in range(rows):
        total = picked(column_ref[:, rows + m : rows + m + 1], come_ref)
        total = (total + kept_ref[m * LANES : (m + 1) * LANES].astype(f32)).astype(bf16)
        for t in range(LANES // half):
            heat_ref[m + rows * t] = total[t * half : (t + 1) * half, :levels]
            moist_ref[m + rows * t] = total[t * half : (t + 1) * half, levels:]


def placed(room, shape, column_plan, pack_plan, result, after):
    packed = pack(room, pack_plan, result, after)
    come = lax.ppermute(packed, "grp", [(0, 1), (1, 0)])
    kept = pl.pallas_call(
        keep_kernel,
        out_shape=jax.ShapeDtypeStruct((shape[0] * shape[1], result.shape[1]), bf16),
        in_specs=[VMEM, VMEM, HBM],
        compiler_params=params(12),
        cost_estimate=cost(2 * shape[0] * shape[1] * result.size, MIB),
        name="keep",
    )(column_plan, result, packed)
    out = jax.ShapeDtypeStruct(shape, bf16)
    return tuple(
        pl.pallas_call(
            place_kernel,
            out_shape=(out, out),
            compiler_params=params(12),
            cost_estimate=cost(2 * shape[0] * shape[1] * come.size, 2 * MIB),
            name="place",
        )(column_plan, kept, come)
    )


def silu(s):
    h = 0.5 * s
    return h + h * jnp.tanh(h)


def layer(source, weight, target):
    total = weight.shape[1]
    tile = min(256, total)
    for i in range(total // tile):
        at = slice(i * tile, (i + 1) * tile)
        sums = jnp.dot(source[...], weight[:, at], preferred_element_type=f32)
        target[:, at] = silu(sums).astype(bf16)


def fetch_kernel(first_in, second_in, _, first_ref, second_ref, sem):
    copies = [
        pltpu.make_async_copy(first_in.at[0], first_ref, sem.at[0]),
        pltpu.make_async_copy(
            second_in.at[0, :, : second_ref.shape[1]], second_ref, sem.at[1]
        ),
    ]
    for copy in copies:
        copy.start()
    for copy in copies:
        copy.wait()


def fetched(first, second, after):
    return pl.pallas_call(
        fetch_kernel,
        out_shape=(
            pltpu.VMEM(first.shape[1:], bf16),
            pltpu.VMEM((second.shape[1], second.shape[2] // 2), bf16),
        ),
        in_specs=[HBM, HBM, VMEM],
        out_specs=(VMEM, VMEM),
        scratch_shapes=[pltpu.SemaphoreType.DMA((2,))],
        compiler_params=params(6),
        cost_estimate=cost(0, 2 * first.size + second.size),
        name="fetch",
    )(*in_hbm(first, second), after)


def front_kernel(x_ref, first_ref, left_ref, second_in, out_ref, one_ref, right_ref, sem):
    near = left_ref.shape[1]
    copy = pltpu.make_async_copy(second_in.at[0, :, near:], right_ref, sem.at[0])
    copy.start()
    layer(x_ref, first_ref, one_ref)
    layer(one_ref, left_ref, out_ref.at[:, :near])
    copy.wait()
    layer(one_ref, right_ref, out_ref.at[:, near:])


def back_kernel(
    two_ref, third_ref, last_ref, _, __, out_hbm, token_ref, three_ref, out_ref, sem
):
    token_ref[...] = jnp.zeros_like(token_ref)
    piece = out_ref.shape[0] // BATCHES
    copies = []
    for i in range(BATCHES):
        at = slice(i * piece, (i + 1) * piece)
        layer(two_ref.at[at], third_ref, three_ref.at[at])
        out_ref[at] = jnp.dot(
            three_ref[at], last_ref[...], preferred_element_type=f32
        ).astype(bf16)
        copies.append(pltpu.make_async_copy(out_ref.at[at], out_hbm.at[at], sem.at[i]))
        copies[-1].start()
    for copy in copies:
        copy.wait()


def front(x, first, left, second):
    rows, hidden = x.shape[0], first.shape[1]
    size = first.size + second.size
    first, left = [pltpu.with_memory_space_constraint(w, pltpu.VMEM) for w in (first, left)]
    return pl.pallas_call(
        front_kernel,
        out_shape=jax.ShapeDtypeStruct((rows, hidden), bf16),
        in_specs=[VMEM] * 3 + [HBM],
        scratch_shapes=[
            pltpu.VMEM((rows, hidden), bf16),
            pltpu.VMEM((second.shape[1], second.shape[2] - left.shape[1]), bf16),
            pltpu.SemaphoreType.DMA((1,)),
        ],
        compiler_params=params(14),
        cost_estimate=cost(2 * rows * size, 2 * size),
        name="front",
    )(x, first, left, *in_hbm(second))


def back(two, third, last, *after):
    rows, hidden = two.shape
    size = third.size + last.size
    return pl.pallas_call(
        back_kernel,
        out_shape=(jax.ShapeDtypeStruct((rows, last.shape[1]), bf16), TOKEN),
        in_specs=[VMEM] * 3 + [ANY] * len(after),
        out_specs=(HBM, VMEM),
        scratch_shapes=[
            pltpu.VMEM((rows, hidden), bf16),
            pltpu.VMEM((rows, last.shape[1]), bf16),
            pltpu.SemaphoreType.DMA((BATCHES,)),
        ],
        compiler_params=params(14),
        cost_estimate=cost(2 * rows * size, 2 * size),
        name="back",
    )(two, third, last, *after)


def dynamics_kernel(
    group_ref, rate_ref, e_hbm, n_hbm, p_hbm, left_in, right_in, _, e_out, n_out, p_out, token_ref,
    e_ref, n_ref, p_ref, e_in, n_in, p_in, left_ref, right_ref, sem,
):
    inputs = [
        pltpu.make_async_copy(source, target, sem.at[2 + i])
        for i, (source, target) in enumerate(((e_hbm, e_in), (n_hbm, n_in), (p_hbm, p_in)))
    ]
    for copy in inputs:
        copy.start()
    sides = [
        pltpu.make_async_copy(left_in, left_ref, sem.at[0]),
        pltpu.make_async_copy(right_in, right_ref, sem.at[1]),
    ]
    for side in sides:
        side.start()
    token_ref[...] = jnp.zeros_like(token_ref)
    deep, half = e_out.shape[:2]
    span = e_ref.shape[1]
    reach = span - half
    wide = e_in.shape[1]
    mine = group_ref[0]
    coef = rate_ref[...] * 0.5

    edge = jnp.zeros((8, LANES), f32)

    for ref in (n_ref, p_ref):

        def clear(i, _, ref=ref):
            ref[i, 0:8] = edge
            ref[i, 8 + span : 16 + span] = edge
            return 0

        lax.fori_loop(0, ref.shape[0], clear, 0)

    fields = (
        (p_in, p_out, p_ref, 8, reach),
        (e_in, e_out, e_ref, 0, reach - 1),
        (n_in, n_out, n_ref, 8, reach - 2),
    )

    for copy in inputs:
        copy.wait()

    def load(i, _):
        for source, _, ref, off, width in fields:
            row = source[i].astype(f32)
            ref[i + width, off : off + span] = jnp.where(
                mine == 0, row[:span], row[wide - span :]
            )
        return 0

    lax.fori_loop(0, deep, load, 0)
    for side in sides:
        side.wait()
    start = 0
    for _, _, ref, off, width in fields:
        for i in range(width):
            ref[i, off : off + span] = left_ref[start + i].astype(f32)
            ref[i + width + deep, off : off + span] = right_ref[start + i].astype(f32)
        start += width

    mid, low, high = slice(8, 8 + span), slice(7, 7 + span), slice(9, 9 + span)

    def wind(i):
        e_ref[i] = e_ref[i] - coef * (p_ref[i + 2, mid] - p_ref[i, mid])

    for s in range(SUB):
        first, last = 2 * s, n_ref.shape[0] - 2 * s
        wind(first)

        def winds(k, _, first=first):
            for i in (first + 2 * k, first + 2 * k + 1):
                wind(i + 1)
                n_ref[i, mid] = n_ref[i, mid] - coef * (p_ref[i + 2, high] - p_ref[i + 2, low])
            return 0

        lax.fori_loop(0, (last - first) // 2, winds, 0)
        wind(last + 1)

        def pressure(k, _, first=first):
            for i in (first + 2 * k, first + 2 * k + 1):
                p_ref[i + 2, mid] = p_ref[i + 2, mid] - coef * (
                    (e_ref[i + 2] - e_ref[i]) + (n_ref[i, high] - n_ref[i, low])
                )
            return 0

        lax.fori_loop(0, (last - first) // 2, pressure, 0)

    def store(i, _):
        for _, out, ref, off, width in fields:
            near = ref[i + width, off : off + half]
            far = ref[i + width, off + reach : off + reach + half]
            out[i] = jnp.where(mine == 0, near, far).astype(bf16)
        return 0

    lax.fori_loop(0, deep, store, 0)


def dynamics(group, rate, e, n, p, left, right, after):
    deep, wide, levels = e.shape
    half = wide // 2
    reach = 2 * SUB
    span = half + reach
    out = jax.ShapeDtypeStruct((deep, half, levels), bf16)
    cells = deep * half * levels
    return pl.pallas_call(
        dynamics_kernel,
        out_shape=(out,) * 3 + (TOKEN,),
        in_specs=[SMEM, VMEM] + [HBM] * 3 + [ANY] * 2 + [VMEM],
        scratch_shapes=[
            pltpu.VMEM((deep + 2 * (reach - 1), span, levels), f32),
            pltpu.VMEM((deep + 2 * (reach - 2), span + 16, levels), f32),
            pltpu.VMEM((deep + 2 * reach, span + 16, levels), f32),
            *[pltpu.VMEM(e.shape, bf16)] * 3,
            pltpu.VMEM(left.shape, bf16),
            pltpu.VMEM(right.shape, bf16),
            pltpu.SemaphoreType.DMA((5,)),
        ],
        compiler_params=params(12),
        cost_estimate=cost(cells * 200, cells * 24),
        name="dynamics",
    )(group, rate, *in_hbm(e, n, p), left, right, after)


def edges_kernel(group_ref, e_in, n_in, p_in, _, tail_ref, head_ref, last_ref, first_ref, sem):
    deep, wide = e_in.shape[:2]
    span = tail_ref.shape[1]
    mine = group_ref[0]
    reach = 2 * SUB
    copies = []
    at = 0
    for source, width in ((p_in, reach), (e_in, reach - 1), (n_in, reach - 2)):
        for target, start in ((last_ref, deep - width), (first_ref, 0)):
            copies.append(
                pltpu.make_async_copy(
                    source.at[start : start + width],
                    target.at[at : at + width],
                    sem.at[len(copies)],
                )
            )
        at += width
    for copy in copies:
        copy.start()
    for copy in copies:
        copy.wait()
    for source, out in ((last_ref, tail_ref), (first_ref, head_ref)):
        for i in range(at):
            whole = source[i].astype(f32)
            out[i] = jnp.where(mine == 0, whole[:span], whole[wide - span :]).astype(bf16)


def halos(group, e, n, p, after):
    wide, levels = e.shape[1:]
    reach = 2 * SUB
    count = lax.axis_size("blk")
    out = jax.ShapeDtypeStruct((3 * reach - 3, wide // 2 + reach, levels), bf16)
    tail, head = pl.pallas_call(
        edges_kernel,
        out_shape=(out, out),
        in_specs=[SMEM] + [HBM] * 3 + [VMEM],
        scratch_shapes=[pltpu.VMEM((3 * reach - 3, wide, levels), bf16)] * 2
        + [pltpu.SemaphoreType.DMA((6,))],
        compiler_params=params(6),
        cost_estimate=cost(MIB, 2 * MIB),
        name="edges",
    )(group, *in_hbm(e, n, p), after)
    left = lax.ppermute(tail, "blk", [(i, (i + 1) % count) for i in range(count)])
    right = lax.ppermute(head, "blk", [((i + 1) % count, i) for i in range(count)])
    return left, right


def local(
    zonal_velocity_field,
    meridional_velocity_field,
    barometric_disturbance,
    delayed_thermal_deviation,
    delayed_moisture_deviation,
    flow_category_label,
    advective_stability_number,
    initial_dense_matrix,
    middle_dense_matrix,
    closing_dense_matrix,
    final_readout_matrix,
):
    group = jnp.full((1,), lax.axis_index("grp"), i32)
    regimes = lax.axis_size("blk")
    deep, wide, levels = zonal_velocity_field.shape
    half = wide // 2
    profile = 2 * levels
    part = deep * wide // regimes // 2
    size = regimes * part
    rows = deep * half // LANES

    def swapped(one):
        one = one.reshape(regimes, part, profile)
        one = lax.all_to_all(one, "blk", split_axis=0, concat_axis=0, tiled=True)
        return one.reshape(size, profile)

    sent, routed = pl.pallas_call(
        functools.partial(route_kernel, regimes, part),
        out_shape=(jax.ShapeDtypeStruct((size, profile), bf16), TOKEN),
        in_specs=[SMEM, HBM, HBM, HBM],
        scratch_shapes=[
            pltpu.VMEM((deep, wide), i32),
            pltpu.VMEM((deep, wide, levels), bf16),
            pltpu.VMEM((deep, wide, levels), bf16),
            pltpu.SemaphoreType.DMA((1 + 2 * (LANES // half),)),
        ],
        compiler_params=params(16),
        cost_estimate=cost(2 * size * deep * wide * profile, 2 * MIB),
        name="route",
    )(
        group,
        *in_hbm(flow_category_label, delayed_thermal_deviation, delayed_moisture_deviation),
    )
    arrived = swapped(sent)
    left, right = halos(
        group, zonal_velocity_field, meridional_velocity_field, barometric_disturbance, routed
    )
    column_plan, pack_plan, crowded = plan(regimes, part, rows, group, flow_category_label, routed)
    two = front(
        arrived,
        *fetched(initial_dense_matrix, middle_dense_matrix, routed),
        middle_dense_matrix,
    )
    result, worked = back(two, closing_dense_matrix[0], final_readout_matrix[0], left, right)
    returned = swapped(result)
    east, north, pressure, moved = dynamics(
        group,
        advective_stability_number.reshape(1, levels),
        zonal_velocity_field,
        meridional_velocity_field,
        barometric_disturbance,
        left,
        right,
        worked,
    )
    shape = (deep, half, levels)
    heating, moistening = lax.cond(
        crowded[0] > 0,
        functools.partial(placed, size // 2, shape),
        functools.partial(placed, min(ROOM, size // 2), shape),
        column_plan,
        pack_plan,
        returned,
        moved,
    )
    return east, north, pressure, heating, moistening


def solution(mesh):
    return jax.shard_map(
        local,
        mesh=mesh,
        in_specs=(P("blk", None, None),) * 5
        + (P("blk", None), P())
        + (P("blk", None, None),) * 4,
        out_specs=(P("blk", "grp", None),) * 5,
        check_vma=False,
    )
```

```python
import functools
import jax
import jax.numpy as jnp
from jax import lax
from jax.experimental import pallas as pl
from jax.experimental.pallas import tpu as pltpu
from jax.sharding import PartitionSpec as P

SUB = 4
BATCHES = 2
ROOM = 80
LANES = 128
MIB = 1 << 20
bf16, f32, i32 = jnp.bfloat16, jnp.float32, jnp.int32
SMEM = pl.BlockSpec(memory_space=pltpu.SMEM)
VMEM = pl.BlockSpec(memory_space=pltpu.VMEM)
HBM = pl.BlockSpec(memory_space=pltpu.HBM)
ANY = pl.BlockSpec(memory_space=pl.ANY)


def params(mib):
    return pltpu.CompilerParams(vmem_limit_bytes=mib * MIB)


TOKEN = jax.ShapeDtypeStruct((8, LANES), f32)


def in_hbm(*arrays):
    return [pltpu.with_memory_space_constraint(x, pltpu.HBM) for x in arrays]


def cost(flops, moved):
    return pl.CostEstimate(flops=flops, bytes_accessed=moved, transcendentals=0)


def folded(label_ref, start, half):
    pieces = LANES // half
    rows = label_ref.shape[0] // pieces
    return jnp.concatenate(
        [
            label_ref[pl.ds(t, rows, stride=pieces), :][:, start : start + half]
            for t in range(pieces)
        ],
        axis=1,
    )


def ranked(labels, regimes):
    rows = labels.shape[0]
    shape = (regimes, rows, LANES)
    member = jnp.where(
        lax.broadcasted_iota(i32, shape, 0) == jnp.broadcast_to(labels[None], shape), 1.0, 0.0
    )
    flat = member.reshape(regimes * rows, LANES).astype(bf16)
    first = lax.broadcasted_iota(i32, (LANES, LANES), 0)
    second = lax.broadcasted_iota(i32, (LANES, LANES), 1)
    earlier = jnp.where(first < second, 1.0, 0.0).astype(bf16)
    totals = jnp.dot(flat, jnp.ones((LANES, LANES), bf16), preferred_element_type=f32)
    within = jnp.dot(flat, earlier, preferred_element_type=f32)
    totals = totals.reshape(shape)
    row = lax.broadcasted_iota(i32, (1, rows, LANES), 1)
    before, step = totals, 1
    while step < rows:
        before = before + jnp.where(row >= step, pltpu.roll(before, step, 1), 0.0)
        step *= 2
    count = before[:, rows - 1 :]
    rank = jnp.sum(member * (within.reshape(shape) + (before - totals)), axis=0)
    return rank, member, count


def route_kernel(
    regimes, part, group_ref, label_in, heat_in, moist_in, out_ref, token_ref, label_ref, heat_ref, moist_ref, sem
):
    token_ref[...] = jnp.zeros_like(token_ref)
    deep, wide, levels = heat_ref.shape
    half = wide // 2
    rows = deep * half // LANES
    pieces = LANES // half
    first = pltpu.make_async_copy(label_in, label_ref, sem.at[0])
    first.start()
    copies = []
    for t in range(pieces):
        at = slice(t * rows, (t + 1) * rows)
        for source, target in ((heat_in, heat_ref), (moist_in, moist_ref)):
            n = len(copies) + 1
            copies.append(pltpu.make_async_copy(source.at[at], target.at[at], sem.at[n]))
            copies[-1].start()
    mine = group_ref[0]
    first.wait()
    targets = []
    for side in range(2):
        index = folded(label_ref, side * half, half)
        rank, _, _ = ranked(index, regimes)
        place = jnp.where(mine == side, part - 1.0 - rank, rank - part)
        targets.append(jnp.where(place >= 0, index.astype(f32) * part + place, -1.0))
    target = jnp.concatenate(targets, axis=0)
    for copy in copies:
        copy.wait()
    columns = []
    for side in range(2):
        for m in range(rows):
            for t in range(pieces):
                at = (m * pieces + t, slice(side * half, (side + 1) * half))
                columns.append(jnp.concatenate([heat_ref[at], moist_ref[at]], axis=1))
    soundings = jnp.concatenate(columns, axis=0)
    total = out_ref.shape[0]
    tile = min(256, total)
    slot = lax.broadcasted_iota(i32, (tile, LANES), 0).astype(f32).astype(bf16)
    yes, no = jnp.ones((), bf16), jnp.zeros((), bf16)
    for start in range(0, total, tile):
        near = target - start
        near = jnp.where((near >= 0) & (near < tile), near, -1.0).astype(bf16)
        picks = jnp.concatenate(
            [jnp.where(slot == near[m : m + 1], yes, no) for m in range(2 * rows)], axis=1
        )
        out_ref[start : start + tile] = jnp.dot(
            picks, soundings, preferred_element_type=f32
        ).astype(bf16)


def plan_kernel(regimes, part, group_ref, label_ref, _, column_ref, pack_ref, crowd_ref):
    half = label_ref.shape[1] // 2
    mine = group_ref[0]
    sides = []
    for side in range(2):
        index = folded(label_ref, side * half, half)
        rank, member, count = ranked(index, regimes)
        sides.append((index.astype(f32), rank, member, jnp.maximum(count - part, 0.0)))
    index, rank, member, spare = [jnp.where(mine == 0, a, b) for a, b in zip(*sides)]
    rows = rank.shape[0]
    offset = jnp.zeros((1, LANES), f32)
    at = jnp.zeros(rank.shape, f32)
    for r in range(regimes):
        at = at + member[r] * offset
        offset = offset + spare[r]
    crowd_ref[0] = (jnp.max(offset) > ROOM).astype(i32)
    kept = jnp.where(rank < part, index * part + (part - 1.0 - rank), -1.0)
    come = jnp.where(rank >= part, at + (rank - part), -1.0)
    column_ref[:, :rows] = kept.T
    column_ref[:, rows : 2 * rows] = come.T
    spare = jnp.where(mine == 0, sides[1][3], sides[0][3])
    lane = lax.broadcasted_iota(i32, (1, LANES), 1)
    offset = jnp.zeros((1, LANES), f32)
    per_row = LANES // part
    for r in range(regimes):
        if r % per_row == 0:
            line = jnp.full((1, LANES), -1.0)
        near = (lane - (r % per_row) * part).astype(f32)
        line = jnp.where((near >= 0) & (near < spare[r]), offset + near, line)
        offset = offset + spare[r]
        if r % per_row == per_row - 1:
            pack_ref[r // per_row : r // per_row + 1] = line


def plan(regimes, part, rows, group, labels, after):
    return pl.pallas_call(
        functools.partial(plan_kernel, regimes, part),
        out_shape=(
            jax.ShapeDtypeStruct((LANES, 2 * rows), f32),
            jax.ShapeDtypeStruct((regimes * part // LANES, LANES), f32),
            jax.ShapeDtypeStruct((1,), i32),
        ),
        in_specs=[SMEM, VMEM, VMEM],
        out_specs=(VMEM, VMEM, SMEM),
        compiler_params=params(12),
        cost_estimate=cost(MIB, MIB),
        name="plan",
    )(group, labels, after)


def pack_kernel(pack_ref, result_ref, _, out_ref):
    slot = lax.broadcasted_iota(i32, (out_ref.shape[0], LANES), 0).astype(f32)
    picks = jnp.concatenate(
        [
            jnp.where(slot == pack_ref[m : m + 1], 1.0, 0.0).astype(bf16)
            for m in range(pack_ref.shape[0])
        ],
        axis=1,
    )
    out_ref[...] = jnp.dot(picks, result_ref[...], preferred_element_type=f32).astype(bf16)


def pack(room, pack_plan, result, after):
    return pl.pallas_call(
        pack_kernel,
        out_shape=jax.ShapeDtypeStruct((room, result.shape[1]), bf16),
        in_specs=[VMEM, VMEM, VMEM],
        compiler_params=params(12),
        cost_estimate=cost(2 * room * result.size, MIB),
        name="pack",
    )(pack_plan, result, after)


def picked(wanted, source_ref):
    slot = lax.broadcasted_iota(i32, (LANES, source_ref.shape[0]), 1).astype(f32)
    picks = jnp.where(slot == wanted, 1.0, 0.0).astype(bf16)
    return jnp.dot(picks, source_ref[...], preferred_element_type=f32)


def keep_kernel(column_ref, result_ref, packed_ref, out_ref):
    del packed_ref
    for m in range(column_ref.shape[1] // 2):
        out_ref[m * LANES : (m + 1) * LANES] = picked(
            column_ref[:, m : m + 1], result_ref
        ).astype(bf16)


def place_kernel(column_ref, kept_ref, come_ref, heat_out, moist_out, heat_ref, moist_ref, sem):
    deep, half, levels = heat_ref.shape
    pieces = LANES // half
    rows = deep // pieces
    copies = []
    for m in range(rows):
        total = picked(column_ref[:, rows + m : rows + m + 1], come_ref)
        total = (total + kept_ref[m * LANES : (m + 1) * LANES].astype(f32)).astype(bf16)
        for t in range(pieces):
            heat_ref[m * pieces + t] = total[t * half : (t + 1) * half, :levels]
            moist_ref[m * pieces + t] = total[t * half : (t + 1) * half, levels:]
        if m % 2 == 1:
            at = slice((m - 1) * pieces, (m + 1) * pieces)
            for source, target in ((heat_ref, heat_out), (moist_ref, moist_out)):
                copy = pltpu.make_async_copy(source.at[at], target.at[at], sem.at[len(copies)])
                copy.start()
                copies.append(copy)
    for copy in copies:
        copy.wait()


def placed(room, shape, column_plan, pack_plan, result, after):
    packed = pack(room, pack_plan, result, after)
    come = lax.ppermute(packed, "grp", [(0, 1), (1, 0)])
    kept = pl.pallas_call(
        keep_kernel,
        out_shape=jax.ShapeDtypeStruct((shape[0] * shape[1], result.shape[1]), bf16),
        in_specs=[VMEM, VMEM, HBM],
        compiler_params=params(12),
        cost_estimate=cost(2 * shape[0] * shape[1] * result.size, MIB),
        name="keep",
    )(column_plan, result, packed)
    out = jax.ShapeDtypeStruct(shape, bf16)
    return tuple(
        pl.pallas_call(
            place_kernel,
            out_shape=(out, out),
            out_specs=(HBM, HBM),
            scratch_shapes=[pltpu.VMEM(shape, bf16)] * 2
            + [pltpu.SemaphoreType.DMA((shape[0] * shape[1] // LANES,))],
            compiler_params=params(12),
            cost_estimate=cost(2 * shape[0] * shape[1] * come.size, 2 * MIB),
            name="place",
        )(column_plan, kept, come)
    )


def silu(s):
    h = 0.5 * s
    return h + h * jnp.tanh(h)


def layer(source, weight, target):
    total = weight.shape[1]
    tile = min(256, total)
    for i in range(total // tile):
        at = slice(i * tile, (i + 1) * tile)
        sums = jnp.dot(source[...], weight[:, at], preferred_element_type=f32)
        target[:, at] = silu(sums).astype(bf16)


def fetch_kernel(first_in, second_in, _, first_ref, second_ref, sem):
    copies = [
        pltpu.make_async_copy(first_in.at[0], first_ref, sem.at[0]),
        pltpu.make_async_copy(
            second_in.at[0, :, : second_ref.shape[1]], second_ref, sem.at[1]
        ),
    ]
    for copy in copies:
        copy.start()
    for copy in copies:
        copy.wait()


def fetched(first, second, after):
    return pl.pallas_call(
        fetch_kernel,
        out_shape=(
            pltpu.VMEM(first.shape[1:], bf16),
            pltpu.VMEM((second.shape[1], second.shape[2] // 2), bf16),
        ),
        in_specs=[HBM, HBM, VMEM],
        out_specs=(VMEM, VMEM),
        scratch_shapes=[pltpu.SemaphoreType.DMA((2,))],
        compiler_params=params(6),
        cost_estimate=cost(0, 2 * first.size + second.size),
        name="fetch",
    )(*in_hbm(first, second), after)


def front_kernel(x_ref, first_ref, left_ref, second_in, out_ref, one_ref, right_ref, sem):
    near = left_ref.shape[1]
    copy = pltpu.make_async_copy(second_in.at[0, :, near:], right_ref, sem.at[0])
    copy.start()
    layer(x_ref, first_ref, one_ref)
    layer(one_ref, left_ref, out_ref.at[:, :near])
    copy.wait()
    layer(one_ref, right_ref, out_ref.at[:, near:])


def back_kernel(
    two_ref, third_ref, last_ref, _, __, out_hbm, token_ref, three_ref, out_ref, sem
):
    token_ref[...] = jnp.zeros_like(token_ref)
    piece = out_ref.shape[0] // BATCHES
    copies = []
    for i in range(BATCHES):
        at = slice(i * piece, (i + 1) * piece)
        layer(two_ref.at[at], third_ref, three_ref.at[at])
        out_ref[at] = jnp.dot(
            three_ref[at], last_ref[...], preferred_element_type=f32
        ).astype(bf16)
        copies.append(pltpu.make_async_copy(out_ref.at[at], out_hbm.at[at], sem.at[i]))
        copies[-1].start()
    for copy in copies:
        copy.wait()


def front(x, first, left, second):
    rows, hidden = x.shape[0], first.shape[1]
    size = first.size + second.size
    first, left = [pltpu.with_memory_space_constraint(w, pltpu.VMEM) for w in (first, left)]
    return pl.pallas_call(
        front_kernel,
        out_shape=jax.ShapeDtypeStruct((rows, hidden), bf16),
        in_specs=[VMEM] * 3 + [HBM],
        scratch_shapes=[
            pltpu.VMEM((rows, hidden), bf16),
            pltpu.VMEM((second.shape[1], second.shape[2] - left.shape[1]), bf16),
            pltpu.SemaphoreType.DMA((1,)),
        ],
        compiler_params=params(14),
        cost_estimate=cost(2 * rows * size, 2 * size),
        name="front",
    )(x, first, left, *in_hbm(second))


def back(two, third, last, *after):
    rows, hidden = two.shape
    size = third.size + last.size
    return pl.pallas_call(
        back_kernel,
        out_shape=(jax.ShapeDtypeStruct((rows, last.shape[1]), bf16), TOKEN),
        in_specs=[VMEM] * 3 + [ANY] * len(after),
        out_specs=(HBM, VMEM),
        scratch_shapes=[
            pltpu.VMEM((rows, hidden), bf16),
            pltpu.VMEM((rows, last.shape[1]), bf16),
            pltpu.SemaphoreType.DMA((BATCHES,)),
        ],
        compiler_params=params(14),
        cost_estimate=cost(2 * rows * size, 2 * size),
        name="back",
    )(two, third, last, *after)


def dynamics_kernel(
    group_ref, rate_ref, e_hbm, n_hbm, p_hbm, left_in, right_in, _, e_out, n_out, p_out, token_ref,
    e_ref, n_ref, p_ref, e_in, n_in, p_in, left_ref, right_ref, sem,
):
    inputs = [
        pltpu.make_async_copy(source, target, sem.at[2 + i])
        for i, (source, target) in enumerate(((e_hbm, e_in), (n_hbm, n_in), (p_hbm, p_in)))
    ]
    for copy in inputs:
        copy.start()
    sides = [
        pltpu.make_async_copy(left_in, left_ref, sem.at[0]),
        pltpu.make_async_copy(right_in, right_ref, sem.at[1]),
    ]
    for side in sides:
        side.start()
    token_ref[...] = jnp.zeros_like(token_ref)
    deep, half = e_out.shape[:2]
    span = e_ref.shape[1]
    reach = span - half
    wide = e_in.shape[1]
    mine = group_ref[0]
    coef = rate_ref[...] * 0.5

    edge = jnp.zeros((8, LANES), f32)

    for ref in (n_ref, p_ref):

        def clear(i, _, ref=ref):
            ref[i, 0:8] = edge
            ref[i, 8 + span : 16 + span] = edge
            return 0

        lax.fori_loop(0, ref.shape[0], clear, 0)

    fields = (
        (p_in, p_out, p_ref, 8, reach),
        (e_in, e_out, e_ref, 0, reach - 1),
        (n_in, n_out, n_ref, 8, reach - 2),
    )

    for copy in inputs:
        copy.wait()

    def load(i, _):
        for source, _, ref, off, width in fields:
            row = source[i].astype(f32)
            ref[i + width, off : off + span] = jnp.where(
                mine == 0, row[:span], row[wide - span :]
            )
        return 0

    lax.fori_loop(0, deep, load, 0)
    for side in sides:
        side.wait()
    start = 0
    for _, _, ref, off, width in fields:
        for i in range(width):
            ref[i, off : off + span] = left_ref[start + i].astype(f32)
            ref[i + width + deep, off : off + span] = right_ref[start + i].astype(f32)
        start += width

    mid, low, high = slice(8, 8 + span), slice(7, 7 + span), slice(9, 9 + span)

    def wind(i):
        e_ref[i] = e_ref[i] - coef * (p_ref[i + 2, mid] - p_ref[i, mid])

    for s in range(SUB):
        first, last = 2 * s, n_ref.shape[0] - 2 * s
        wind(first)

        def winds(k, _, first=first):
            for i in (first + 2 * k, first + 2 * k + 1):
                wind(i + 1)
                n_ref[i, mid] = n_ref[i, mid] - coef * (p_ref[i + 2, high] - p_ref[i + 2, low])
            return 0

        lax.fori_loop(0, (last - first) // 2, winds, 0)
        wind(last + 1)

        def pressure(k, _, first=first):
            for i in (first + 2 * k, first + 2 * k + 1):
                p_ref[i + 2, mid] = p_ref[i + 2, mid] - coef * (
                    (e_ref[i + 2] - e_ref[i]) + (n_ref[i, high] - n_ref[i, low])
                )
            return 0

        lax.fori_loop(0, (last - first) // 2, pressure, 0)

    def store(i, _):
        for _, out, ref, off, width in fields:
            near = ref[i + width, off : off + half]
            far = ref[i + width, off + reach : off + reach + half]
            out[i] = jnp.where(mine == 0, near, far).astype(bf16)
        return 0

    lax.fori_loop(0, deep, store, 0)


def dynamics(group, rate, e, n, p, left, right, after):
    deep, wide, levels = e.shape
    half = wide // 2
    reach = 2 * SUB
    span = half + reach
    out = jax.ShapeDtypeStruct((deep, half, levels), bf16)
    cells = deep * half * levels
    return pl.pallas_call(
        dynamics_kernel,
        out_shape=(out,) * 3 + (TOKEN,),
        in_specs=[SMEM, VMEM] + [HBM] * 3 + [ANY] * 2 + [VMEM],
        scratch_shapes=[
            pltpu.VMEM((deep + 2 * (reach - 1), span, levels), f32),
            pltpu.VMEM((deep + 2 * (reach - 2), span + 16, levels), f32),
            pltpu.VMEM((deep + 2 * reach, span + 16, levels), f32),
            *[pltpu.VMEM(e.shape, bf16)] * 3,
            pltpu.VMEM(left.shape, bf16),
            pltpu.VMEM(right.shape, bf16),
            pltpu.SemaphoreType.DMA((5,)),
        ],
        compiler_params=params(12),
        cost_estimate=cost(cells * 200, cells * 24),
        name="dynamics",
    )(group, rate, *in_hbm(e, n, p), left, right, after)


def edges_kernel(group_ref, e_in, n_in, p_in, _, tail_ref, head_ref, last_ref, first_ref, sem):
    deep, wide = e_in.shape[:2]
    span = tail_ref.shape[1]
    mine = group_ref[0]
    reach = 2 * SUB
    copies = []
    at = 0
    for source, width in ((p_in, reach), (e_in, reach - 1), (n_in, reach - 2)):
        for target, start in ((last_ref, deep - width), (first_ref, 0)):
            copies.append(
                pltpu.make_async_copy(
                    source.at[start : start + width],
                    target.at[at : at + width],
                    sem.at[len(copies)],
                )
            )
        at += width
    for copy in copies:
        copy.start()
    for copy in copies:
        copy.wait()
    for source, out in ((last_ref, tail_ref), (first_ref, head_ref)):
        for i in range(at):
            whole = source[i].astype(f32)
            out[i] = jnp.where(mine == 0, whole[:span], whole[wide - span :]).astype(bf16)


def halos(group, e, n, p, after):
    wide, levels = e.shape[1:]
    reach = 2 * SUB
    count = lax.axis_size("blk")
    out = jax.ShapeDtypeStruct((3 * reach - 3, wide // 2 + reach, levels), bf16)
    tail, head = pl.pallas_call(
        edges_kernel,
        out_shape=(out, out),
        in_specs=[SMEM] + [HBM] * 3 + [VMEM],
        scratch_shapes=[pltpu.VMEM((3 * reach - 3, wide, levels), bf16)] * 2
        + [pltpu.SemaphoreType.DMA((6,))],
        compiler_params=params(6),
        cost_estimate=cost(MIB, 2 * MIB),
        name="edges",
    )(group, *in_hbm(e, n, p), after)
    left = lax.ppermute(tail, "blk", [(i, (i + 1) % count) for i in range(count)])
    right = lax.ppermute(head, "blk", [((i + 1) % count, i) for i in range(count)])
    return left, right


def local(
    zonal_velocity_field,
    meridional_velocity_field,
    barometric_disturbance,
    delayed_thermal_deviation,
    delayed_moisture_deviation,
    flow_category_label,
    advective_stability_number,
    initial_dense_matrix,
    middle_dense_matrix,
    closing_dense_matrix,
    final_readout_matrix,
):
    group = jnp.full((1,), lax.axis_index("grp"), i32)
    regimes = lax.axis_size("blk")
    deep, wide, levels = zonal_velocity_field.shape
    half = wide // 2
    profile = 2 * levels
    part = deep * wide // regimes // 2
    size = regimes * part
    rows = deep * half // LANES

    def swapped(one):
        one = one.reshape(regimes, part, profile)
        one = lax.all_to_all(one, "blk", split_axis=0, concat_axis=0, tiled=True)
        return one.reshape(size, profile)

    sent, routed = pl.pallas_call(
        functools.partial(route_kernel, regimes, part),
        out_shape=(jax.ShapeDtypeStruct((size, profile), bf16), TOKEN),
        in_specs=[SMEM, HBM, HBM, HBM],
        scratch_shapes=[
            pltpu.VMEM((deep, wide), i32),
            pltpu.VMEM((deep, wide, levels), bf16),
            pltpu.VMEM((deep, wide, levels), bf16),
            pltpu.SemaphoreType.DMA((1 + 2 * (LANES // half),)),
        ],
        compiler_params=params(16),
        cost_estimate=cost(2 * size * deep * wide * profile, 2 * MIB),
        name="route",
    )(
        group,
        *in_hbm(flow_category_label, delayed_thermal_deviation, delayed_moisture_deviation),
    )
    arrived = swapped(sent)
    left, right = halos(
        group, zonal_velocity_field, meridional_velocity_field, barometric_disturbance, routed
    )
    column_plan, pack_plan, crowded = plan(regimes, part, rows, group, flow_category_label, routed)
    two = front(
        arrived,
        *fetched(initial_dense_matrix, middle_dense_matrix, routed),
        middle_dense_matrix,
    )
    result, worked = back(two, closing_dense_matrix[0], final_readout_matrix[0], left, right)
    returned = swapped(result)
    east, north, pressure, moved = dynamics(
        group,
        advective_stability_number.reshape(1, levels),
        zonal_velocity_field,
        meridional_velocity_field,
        barometric_disturbance,
        left,
        right,
        worked,
    )
    shape = (deep, half, levels)
    heating, moistening = lax.cond(
        crowded[0] > 0,
        functools.partial(placed, size // 2, shape),
        functools.partial(placed, min(ROOM, size // 2), shape),
        column_plan,
        pack_plan,
        returned,
        moved,
    )
    return east, north, pressure, heating, moistening


def solution(mesh):
    return jax.shard_map(
        local,
        mesh=mesh,
        in_specs=(P("blk", None, None),) * 5
        + (P("blk", None), P())
        + (P("blk", None, None),) * 4,
        out_specs=(P("blk", "grp", None),) * 5,
        check_vma=False,
    )
```

```python
import functools
import jax
import jax.numpy as jnp
from jax import lax
from jax.experimental import pallas as pl
from jax.experimental.pallas import tpu as pltpu
from jax.sharding import PartitionSpec as P

SUB = 4
BATCHES = 2
ROOM = 80
LANES = 128
MIB = 1 << 20
bf16, f32, i32 = jnp.bfloat16, jnp.float32, jnp.int32
SMEM = pl.BlockSpec(memory_space=pltpu.SMEM)
VMEM = pl.BlockSpec(memory_space=pltpu.VMEM)
HBM = pl.BlockSpec(memory_space=pltpu.HBM)
ANY = pl.BlockSpec(memory_space=pl.ANY)


def params(mib):
    return pltpu.CompilerParams(vmem_limit_bytes=mib * MIB)


TOKEN = jax.ShapeDtypeStruct((8, LANES), f32)


def in_hbm(*arrays):
    return [pltpu.with_memory_space_constraint(x, pltpu.HBM) for x in arrays]


def cost(flops, moved):
    return pl.CostEstimate(flops=flops, bytes_accessed=moved, transcendentals=0)


def folded(label_ref, start, half):
    pieces = LANES // half
    rows = label_ref.shape[0] // pieces
    return jnp.concatenate(
        [
            label_ref[pl.ds(t, rows, stride=pieces), :][:, start : start + half]
            for t in range(pieces)
        ],
        axis=1,
    )


def ranked(labels, regimes):
    rows = labels.shape[0]
    shape = (regimes, rows, LANES)
    member = jnp.where(
        lax.broadcasted_iota(i32, shape, 0) == jnp.broadcast_to(labels[None], shape), 1.0, 0.0
    )
    flat = member.reshape(regimes * rows, LANES).astype(bf16)
    first = lax.broadcasted_iota(i32, (LANES, LANES), 0)
    second = lax.broadcasted_iota(i32, (LANES, LANES), 1)
    earlier = jnp.where(first < second, 1.0, 0.0).astype(bf16)
    totals = jnp.dot(flat, jnp.ones((LANES, LANES), bf16), preferred_element_type=f32)
    within = jnp.dot(flat, earlier, preferred_element_type=f32)
    totals = totals.reshape(shape)
    row = lax.broadcasted_iota(i32, (1, rows, LANES), 1)
    before, step = totals, 1
    while step < rows:
        before = before + jnp.where(row >= step, pltpu.roll(before, step, 1), 0.0)
        step *= 2
    count = before[:, rows - 1 :]
    rank = jnp.sum(member * (within.reshape(shape) + (before - totals)), axis=0)
    return rank, member, count


def route_kernel(
    regimes, part, label_in, heat_in, moist_in, out_hbm, token_ref, label_ref, heat_ref, moist_ref, out_ref, sem, out_sem
):
    token_ref[...] = jnp.zeros_like(token_ref)
    deep, wide, levels = heat_ref.shape
    half = wide // 2
    rows = deep * half // LANES
    pieces = LANES // half
    first = pltpu.make_async_copy(label_in, label_ref, sem.at[0])
    first.start()
    copies = []
    for t in range(pieces):
        at = slice(t * rows, (t + 1) * rows)
        for source, target in ((heat_in, heat_ref), (moist_in, moist_ref)):
            n = len(copies) + 1
            copies.append(pltpu.make_async_copy(source.at[at], target.at[at], sem.at[n]))
            copies[-1].start()
    mine = lax.axis_index("grp")
    first.wait()
    targets = []
    for side in range(2):
        index = folded(label_ref, side * half, half)
        rank, _, _ = ranked(index, regimes)
        place = jnp.where(mine == side, part - 1.0 - rank, rank - part)
        targets.append(jnp.where(place >= 0, index.astype(f32) * part + place, -1.0))
    target = jnp.concatenate(targets, axis=0)
    for copy in copies:
        copy.wait()
    columns = []
    for side in range(2):
        for m in range(rows):
            for t in range(pieces):
                at = (m * pieces + t, slice(side * half, (side + 1) * half))
                columns.append(jnp.concatenate([heat_ref[at], moist_ref[at]], axis=1))
    soundings = jnp.concatenate(columns, axis=0)
    total = out_ref.shape[0]
    tile = min(256, total)
    slot = lax.broadcasted_iota(i32, (tile, LANES), 0).astype(f32).astype(bf16)
    yes, no = jnp.ones((), bf16), jnp.zeros((), bf16)
    sends = []
    for start in range(0, total, tile):
        near = target - start
        near = jnp.where((near >= 0) & (near < tile), near, -1.0).astype(bf16)
        picks = jnp.concatenate(
            [jnp.where(slot == near[m : m + 1], yes, no) for m in range(2 * rows)], axis=1
        )
        out_ref[start : start + tile] = jnp.dot(
            picks, soundings, preferred_element_type=f32
        ).astype(bf16)
        at = slice(start, start + tile)
        sends.append(pltpu.make_async_copy(out_ref.at[at], out_hbm.at[at], out_sem.at[start // tile]))
        sends[-1].start()
    for send in sends:
        send.wait()


def plan_kernel(regimes, part, label_ref, _, column_ref, pack_ref, crowd_ref):
    half = label_ref.shape[1] // 2
    mine = lax.axis_index("grp")
    sides = []
    for side in range(2):
        index = folded(label_ref, side * half, half)
        rank, member, count = ranked(index, regimes)
        sides.append((index.astype(f32), rank, member, jnp.maximum(count - part, 0.0)))
    index, rank, member, spare = [jnp.where(mine == 0, a, b) for a, b in zip(*sides)]
    rows = rank.shape[0]
    offset = jnp.zeros((1, LANES), f32)
    at = jnp.zeros(rank.shape, f32)
    for r in range(regimes):
        at = at + member[r] * offset
        offset = offset + spare[r]
    crowd_ref[0] = (jnp.max(offset) > ROOM).astype(i32)
    kept = jnp.where(rank < part, index * part + (part - 1.0 - rank), -1.0)
    come = jnp.where(rank >= part, at + (rank - part), -1.0)
    column_ref[:, :rows] = kept.T
    column_ref[:, rows : 2 * rows] = come.T
    spare = jnp.where(mine == 0, sides[1][3], sides[0][3])
    lane = lax.broadcasted_iota(i32, (1, LANES), 1)
    offset = jnp.zeros((1, LANES), f32)
    per_row = LANES // part
    for r in range(regimes):
        if r % per_row == 0:
            line = jnp.full((1, LANES), -1.0)
        near = (lane - (r % per_row) * part).astype(f32)
        line = jnp.where((near >= 0) & (near < spare[r]), offset + near, line)
        offset = offset + spare[r]
        if r % per_row == per_row - 1:
            pack_ref[r // per_row : r // per_row + 1] = line


def plan(regimes, part, rows, labels, after):
    return pl.pallas_call(
        functools.partial(plan_kernel, regimes, part),
        out_shape=(
            jax.ShapeDtypeStruct((LANES, 2 * rows), f32),
            jax.ShapeDtypeStruct((regimes * part // LANES, LANES), f32),
            jax.ShapeDtypeStruct((1,), i32),
        ),
        in_specs=[VMEM, VMEM],
        out_specs=(VMEM, VMEM, SMEM),
        compiler_params=params(12),
        cost_estimate=cost(MIB, MIB),
        name="plan",
    )(labels, after)


def pack_kernel(pack_ref, result_ref, _, out_ref):
    slot = lax.broadcasted_iota(i32, (out_ref.shape[0], LANES), 0).astype(f32)
    picks = jnp.concatenate(
        [
            jnp.where(slot == pack_ref[m : m + 1], 1.0, 0.0).astype(bf16)
            for m in range(pack_ref.shape[0])
        ],
        axis=1,
    )
    out_ref[...] = jnp.dot(picks, result_ref[...], preferred_element_type=f32).astype(bf16)


def pack(room, pack_plan, result, after):
    return pl.pallas_call(
        pack_kernel,
        out_shape=jax.ShapeDtypeStruct((room, result.shape[1]), bf16),
        in_specs=[VMEM, VMEM, VMEM],
        compiler_params=params(12),
        cost_estimate=cost(2 * room * result.size, MIB),
        name="pack",
    )(pack_plan, result, after)


def picked(wanted, source_ref):
    slot = lax.broadcasted_iota(i32, (LANES, source_ref.shape[0]), 1).astype(f32)
    picks = jnp.where(slot == wanted, 1.0, 0.0).astype(bf16)
    return jnp.dot(picks, source_ref[...], preferred_element_type=f32)


def keep_kernel(column_ref, result_ref, packed_ref, out_ref):
    del packed_ref
    for m in range(column_ref.shape[1] // 2):
        out_ref[m * LANES : (m + 1) * LANES] = picked(
            column_ref[:, m : m + 1], result_ref
        ).astype(bf16)


def place_kernel(column_ref, kept_ref, come_ref, heat_out, moist_out, heat_ref, moist_ref, sem):
    deep, half, levels = heat_ref.shape
    pieces = LANES // half
    rows = deep // pieces
    copies = []
    for m in range(rows):
        total = picked(column_ref[:, rows + m : rows + m + 1], come_ref)
        total = (total + kept_ref[m * LANES : (m + 1) * LANES].astype(f32)).astype(bf16)
        for t in range(pieces):
            heat_ref[m * pieces + t] = total[t * half : (t + 1) * half, :levels]
            moist_ref[m * pieces + t] = total[t * half : (t + 1) * half, levels:]
        if m % 2 == 1:
            at = slice((m - 1) * pieces, (m + 1) * pieces)
            for source, target in ((heat_ref, heat_out), (moist_ref, moist_out)):
                copy = pltpu.make_async_copy(source.at[at], target.at[at], sem.at[len(copies)])
                copy.start()
                copies.append(copy)
    for copy in copies:
        copy.wait()


def placed(room, shape, column_plan, pack_plan, result, after):
    packed = pack(room, pack_plan, result, after)
    come = lax.ppermute(packed, "grp", [(0, 1), (1, 0)])
    kept = pl.pallas_call(
        keep_kernel,
        out_shape=jax.ShapeDtypeStruct((shape[0] * shape[1], result.shape[1]), bf16),
        in_specs=[VMEM, VMEM, HBM],
        compiler_params=params(12),
        cost_estimate=cost(2 * shape[0] * shape[1] * result.size, MIB),
        name="keep",
    )(column_plan, result, packed)
    out = jax.ShapeDtypeStruct(shape, bf16)
    return tuple(
        pl.pallas_call(
            place_kernel,
            out_shape=(out, out),
            out_specs=(HBM, HBM),
            scratch_shapes=[pltpu.VMEM(shape, bf16)] * 2
            + [pltpu.SemaphoreType.DMA((shape[0] * shape[1] // LANES,))],
            compiler_params=params(12),
            cost_estimate=cost(2 * shape[0] * shape[1] * come.size, 2 * MIB),
            name="place",
        )(column_plan, kept, come)
    )


def silu(s):
    h = 0.5 * s
    return h + h * jnp.tanh(h)


def layer(source, weight, target):
    total = weight.shape[1]
    tile = min(256, total)
    for i in range(total // tile):
        at = slice(i * tile, (i + 1) * tile)
        sums = jnp.dot(source[...], weight[:, at], preferred_element_type=f32)
        target[:, at] = silu(sums).astype(bf16)


def fetch_kernel(first_in, second_in, _, first_ref, second_ref, sem):
    copies = [
        pltpu.make_async_copy(first_in.at[0], first_ref, sem.at[0]),
        pltpu.make_async_copy(
            second_in.at[0, :, : second_ref.shape[1]], second_ref, sem.at[1]
        ),
    ]
    for copy in copies:
        copy.start()
    for copy in copies:
        copy.wait()


def fetched(first, second, after):
    return pl.pallas_call(
        fetch_kernel,
        out_shape=(
            pltpu.VMEM(first.shape[1:], bf16),
            pltpu.VMEM((second.shape[1], second.shape[2] // 2), bf16),
        ),
        in_specs=[HBM, HBM, VMEM],
        out_specs=(VMEM, VMEM),
        scratch_shapes=[pltpu.SemaphoreType.DMA((2,))],
        compiler_params=params(6),
        cost_estimate=cost(0, 2 * first.size + second.size),
        name="fetch",
    )(*in_hbm(first, second), after)


def front_kernel(x_ref, first_ref, left_ref, second_in, out_ref, one_ref, right_ref, sem):
    near = left_ref.shape[1]
    copy = pltpu.make_async_copy(second_in.at[0, :, near:], right_ref, sem.at[0])
    copy.start()
    layer(x_ref, first_ref, one_ref)
    layer(one_ref, left_ref, out_ref.at[:, :near])
    copy.wait()
    layer(one_ref, right_ref, out_ref.at[:, near:])


def back_kernel(
    two_ref, third_ref, last_ref, _, __, out_hbm, token_ref, three_ref, out_ref, sem
):
    token_ref[...] = jnp.zeros_like(token_ref)
    piece = out_ref.shape[0] // BATCHES
    copies = []
    for i in range(BATCHES):
        at = slice(i * piece, (i + 1) * piece)
        layer(two_ref.at[at], third_ref, three_ref.at[at])
        out_ref[at] = jnp.dot(
            three_ref[at], last_ref[...], preferred_element_type=f32
        ).astype(bf16)
        copies.append(pltpu.make_async_copy(out_ref.at[at], out_hbm.at[at], sem.at[i]))
        copies[-1].start()
    for copy in copies:
        copy.wait()


def front(x, first, left, second):
    rows, hidden = x.shape[0], first.shape[1]
    size = first.size + second.size
    first, left = [pltpu.with_memory_space_constraint(w, pltpu.VMEM) for w in (first, left)]
    return pl.pallas_call(
        front_kernel,
        out_shape=jax.ShapeDtypeStruct((rows, hidden), bf16),
        in_specs=[VMEM] * 3 + [HBM],
        scratch_shapes=[
            pltpu.VMEM((rows, hidden), bf16),
            pltpu.VMEM((second.shape[1], second.shape[2] - left.shape[1]), bf16),
            pltpu.SemaphoreType.DMA((1,)),
        ],
        compiler_params=params(14),
        cost_estimate=cost(2 * rows * size, 2 * size),
        name="front",
    )(x, first, left, *in_hbm(second))


def back(two, third, last, *after):
    rows, hidden = two.shape
    size = third.size + last.size
    return pl.pallas_call(
        back_kernel,
        out_shape=(jax.ShapeDtypeStruct((rows, last.shape[1]), bf16), TOKEN),
        in_specs=[VMEM] * 3 + [ANY] * len(after),
        out_specs=(HBM, VMEM),
        scratch_shapes=[
            pltpu.VMEM((rows, hidden), bf16),
            pltpu.VMEM((rows, last.shape[1]), bf16),
            pltpu.SemaphoreType.DMA((BATCHES,)),
        ],
        compiler_params=params(14),
        cost_estimate=cost(2 * rows * size, 2 * size),
        name="back",
    )(two, third, last, *after)


def dynamics_kernel(
    rate_ref, e_hbm, n_hbm, p_hbm, left_in, right_in, _, e_out, n_out, p_out, token_ref,
    e_ref, n_ref, p_ref, e_in, n_in, p_in, left_ref, right_ref, sem,
):
    inputs = [
        pltpu.make_async_copy(source, target, sem.at[2 + i])
        for i, (source, target) in enumerate(((e_hbm, e_in), (n_hbm, n_in), (p_hbm, p_in)))
    ]
    for copy in inputs:
        copy.start()
    sides = [
        pltpu.make_async_copy(left_in, left_ref, sem.at[0]),
        pltpu.make_async_copy(right_in, right_ref, sem.at[1]),
    ]
    for side in sides:
        side.start()
    token_ref[...] = jnp.zeros_like(token_ref)
    deep, half = e_out.shape[:2]
    span = e_ref.shape[1]
    reach = span - half
    wide = e_in.shape[1]
    mine = lax.axis_index("grp")
    coef = rate_ref[...] * 0.5

    edge = jnp.zeros((8, LANES), f32)

    for ref in (n_ref, p_ref):

        def clear(i, _, ref=ref):
            ref[i, 0:8] = edge
            ref[i, 8 + span : 16 + span] = edge
            return 0

        lax.fori_loop(0, ref.shape[0], clear, 0)

    fields = (
        (p_in, p_out, p_ref, 8, reach),
        (e_in, e_out, e_ref, 0, reach - 1),
        (n_in, n_out, n_ref, 8, reach - 2),
    )

    for copy in inputs:
        copy.wait()

    def load(i, _):
        for source, _, ref, off, width in fields:
            row = source[i].astype(f32)
            ref[i + width, off : off + span] = jnp.where(
                mine == 0, row[:span], row[wide - span :]
            )
        return 0

    lax.fori_loop(0, deep, load, 0)
    for side in sides:
        side.wait()
    start = 0
    for _, _, ref, off, width in fields:
        for i in range(width):
            ref[i, off : off + span] = left_ref[start + i].astype(f32)
            ref[i + width + deep, off : off + span] = right_ref[start + i].astype(f32)
        start += width

    mid, low, high = slice(8, 8 + span), slice(7, 7 + span), slice(9, 9 + span)

    def wind(i):
        e_ref[i] = e_ref[i] - coef * (p_ref[i + 2, mid] - p_ref[i, mid])

    for s in range(SUB):
        first, last = 2 * s, n_ref.shape[0] - 2 * s
        wind(first)

        def winds(k, _, first=first):
            for i in (first + 2 * k, first + 2 * k + 1):
                wind(i + 1)
                n_ref[i, mid] = n_ref[i, mid] - coef * (p_ref[i + 2, high] - p_ref[i + 2, low])
            return 0

        lax.fori_loop(0, (last - first) // 2, winds, 0)
        wind(last + 1)

        def pressure(k, _, first=first):
            for i in (first + 2 * k, first + 2 * k + 1):
                p_ref[i + 2, mid] = p_ref[i + 2, mid] - coef * (
                    (e_ref[i + 2] - e_ref[i]) + (n_ref[i, high] - n_ref[i, low])
                )
            return 0

        lax.fori_loop(0, (last - first) // 2, pressure, 0)

    def store(i, _):
        for _, out, ref, off, width in fields:
            near = ref[i + width, off : off + half]
            far = ref[i + width, off + reach : off + reach + half]
            out[i] = jnp.where(mine == 0, near, far).astype(bf16)
        return 0

    lax.fori_loop(0, deep, store, 0)


def dynamics(rate, e, n, p, left, right, after):
    deep, wide, levels = e.shape
    half = wide // 2
    reach = 2 * SUB
    span = half + reach
    out = jax.ShapeDtypeStruct((deep, half, levels), bf16)
    cells = deep * half * levels
    return pl.pallas_call(
        dynamics_kernel,
        out_shape=(out,) * 3 + (TOKEN,),
        in_specs=[VMEM] + [HBM] * 3 + [ANY] * 2 + [VMEM],
        scratch_shapes=[
            pltpu.VMEM((deep + 2 * (reach - 1), span, levels), f32),
            pltpu.VMEM((deep + 2 * (reach - 2), span + 16, levels), f32),
            pltpu.VMEM((deep + 2 * reach, span + 16, levels), f32),
            *[pltpu.VMEM(e.shape, bf16)] * 3,
            pltpu.VMEM(left.shape, bf16),
            pltpu.VMEM(right.shape, bf16),
            pltpu.SemaphoreType.DMA((5,)),
        ],
        compiler_params=params(12),
        cost_estimate=cost(cells * 200, cells * 24),
        name="dynamics",
    )(rate, *in_hbm(e, n, p), left, right, after)


def edges_kernel(e_in, n_in, p_in, _, tail_ref, head_ref, last_ref, first_ref, sem):
    deep, wide = e_in.shape[:2]
    span = tail_ref.shape[1]
    mine = lax.axis_index("grp")
    reach = 2 * SUB
    copies = []
    at = 0
    for source, width in ((p_in, reach), (e_in, reach - 1), (n_in, reach - 2)):
        for target, start in ((last_ref, deep - width), (first_ref, 0)):
            copies.append(
                pltpu.make_async_copy(
                    source.at[start : start + width],
                    target.at[at : at + width],
                    sem.at[len(copies)],
                )
            )
        at += width
    for copy in copies:
        copy.start()
    for copy in copies:
        copy.wait()
    for source, out in ((last_ref, tail_ref), (first_ref, head_ref)):
        for i in range(at):
            whole = source[i].astype(f32)
            out[i] = jnp.where(mine == 0, whole[:span], whole[wide - span :]).astype(bf16)


def halos(e, n, p, after):
    wide, levels = e.shape[1:]
    reach = 2 * SUB
    count = lax.axis_size("blk")
    out = jax.ShapeDtypeStruct((3 * reach - 3, wide // 2 + reach, levels), bf16)
    tail, head = pl.pallas_call(
        edges_kernel,
        out_shape=(out, out),
        in_specs=[HBM] * 3 + [VMEM],
        scratch_shapes=[pltpu.VMEM((3 * reach - 3, wide, levels), bf16)] * 2
        + [pltpu.SemaphoreType.DMA((6,))],
        compiler_params=params(6),
        cost_estimate=cost(MIB, 2 * MIB),
        name="edges",
    )(*in_hbm(e, n, p), after)
    left = lax.ppermute(tail, "blk", [(i, (i + 1) % count) for i in range(count)])
    right = lax.ppermute(head, "blk", [((i + 1) % count, i) for i in range(count)])
    return left, right


def local(
    zonal_velocity_field,
    meridional_velocity_field,
    barometric_disturbance,
    delayed_thermal_deviation,
    delayed_moisture_deviation,
    flow_category_label,
    advective_stability_number,
    initial_dense_matrix,
    middle_dense_matrix,
    closing_dense_matrix,
    final_readout_matrix,
):
    regimes = lax.axis_size("blk")
    deep, wide, levels = zonal_velocity_field.shape
    half = wide // 2
    profile = 2 * levels
    part = deep * wide // regimes // 2
    size = regimes * part
    rows = deep * half // LANES

    def swapped(one):
        one = one.reshape(regimes, part, profile)
        one = lax.all_to_all(one, "blk", split_axis=0, concat_axis=0, tiled=True)
        return one.reshape(size, profile)

    sent, routed = pl.pallas_call(
        functools.partial(route_kernel, regimes, part),
        out_shape=(jax.ShapeDtypeStruct((size, profile), bf16), TOKEN),
        in_specs=[HBM, HBM, HBM],
        out_specs=(HBM, VMEM),
        scratch_shapes=[
            pltpu.VMEM((deep, wide), i32),
            pltpu.VMEM((deep, wide, levels), bf16),
            pltpu.VMEM((deep, wide, levels), bf16),
            pltpu.VMEM((size, profile), bf16),
            pltpu.SemaphoreType.DMA((1 + 2 * (LANES // half),)),
            pltpu.SemaphoreType.DMA((-(-size // 256),)),
        ],
        compiler_params=params(16),
        cost_estimate=cost(2 * size * deep * wide * profile, 2 * MIB),
        name="route",
    )(
        *in_hbm(flow_category_label, delayed_thermal_deviation, delayed_moisture_deviation),
    )
    arrived = swapped(sent)
    left, right = halos(
        zonal_velocity_field, meridional_velocity_field, barometric_disturbance, routed
    )
    column_plan, pack_plan, crowded = plan(regimes, part, rows, flow_category_label, routed)
    two = front(
        arrived,
        *fetched(initial_dense_matrix, middle_dense_matrix, routed),
        middle_dense_matrix,
    )
    result, worked = back(two, closing_dense_matrix[0], final_readout_matrix[0], left, right)
    returned = swapped(result)
    east, north, pressure, moved = dynamics(
        advective_stability_number.reshape(1, levels),
        zonal_velocity_field,
        meridional_velocity_field,
        barometric_disturbance,
        left,
        right,
        worked,
    )
    shape = (deep, half, levels)
    heating, moistening = lax.cond(
        crowded[0] > 0,
        functools.partial(placed, size // 2, shape),
        functools.partial(placed, min(ROOM, size // 2), shape),
        column_plan,
        pack_plan,
        returned,
        moved,
    )
    return east, north, pressure, heating, moistening


def solution(mesh):
    return jax.shard_map(
        local,
        mesh=mesh,
        in_specs=(P("blk", None, None),) * 5
        + (P("blk", None), P())
        + (P("blk", None, None),) * 4,
        out_specs=(P("blk", "grp", None),) * 5,
        check_vma=False,
    )
```
